32 devices in a mesh: survey: 2 (over x), pole: 2 (over core), space: 8 (over z, y).
Axes of the slice: x: 2, y: 2, z: 4, core: 2. Of those that a mesh axis runs over, the one named last changes fastest.
Arguments:
- conductivity: float32 [64, 64, 128], P(('survey', 'space')), parts along dimension 0, may hold values from 0.3 to 9
- source_field: float32 [3, 64, 64, 128], P(None, ('survey', 'space')), parts along dimension 1, may hold values from -6 to 6
- shifts: float32 [8], replicated, may hold values from 1 to 10
- residues: float32 [12, 8], replicated, may hold values from -4 to 4
- receivers: int32 [512], P('survey'), parts along dimension 0, may hold values from 0 to 262143
Outputs:
- gated_field: float32 [12, 3, 64, 64, 128], P(None, None, ('survey', 'space'), 'pole'), parts along dimension 2
- traces: float32 [12, 3, 512], P(None, None, 'survey'), parts along dimension 2
The draws below stay inside these ranges and needn't reach their ends.
There are 2 independent parts, one for each index of `survey`. The reference program is written for one: setup_inputs(seed, part) draws one part's arguments, and reference() takes and returns one part's arrays. A program takes and returns all parts, laid end to end along the dimension named above; an argument that names none is the same for every part. Nothing has to cross between parts.
All inputs are finite; a program needn't handle non-finite values.
Results may differ from the reference program's by a relative error of at most 0.000084.
Values sent between devices are 32-bit elements; how exact they have to be, the bound alone decides.
No kernel may reach another device: no remote copies, remote signals or barrier semaphores. Data moves between devices by JAX's collectives and lax.ppermute only.
A program may use at most 128 MiB of HBM per device.

```python
import math
import jax
import jax.numpy as jnp
from jax import lax

CX = 4
NY = 64
NZ = 128
ITERS = 3
GATES = 12
REC = 256
POLES = 8
NX = 32


def draw_conductivity(key, part):
    ends = jax.random.uniform(jax.random.fold_in(key, 5), (4,), jnp.float32)
    least_value = 0.3 + 0.5 * ends[0]
    most_value = 5.0 + 4.0 * ends[1]
    bulk_low = least_value * (1.3 + 1.2 * ends[2])
    bulk_high = most_value * (0.45 + 0.35 * ends[3])
    roughness = jax.random.uniform(jax.random.fold_in(key, 17), (NX, NY, NZ), jnp.float32)
    block_levels = jax.random.uniform(jax.random.fold_in(key, 23), (NX // CX,), jnp.float32)
    block_line = jnp.repeat(block_levels, CX).reshape(-1, 1, 1)
    trend_line = (jnp.arange(NX, dtype=jnp.float32) / (NX - 1)).reshape(-1, 1, 1)
    mixture = 0.2 * trend_line + 0.35 * block_line + 0.45 * roughness
    values = bulk_low * jnp.exp(mixture * jnp.log(bulk_high / bulk_low))
    total_cells = NX * NY * NZ
    spots = jax.random.randint(jax.random.fold_in(key, 29), (2,), 0, total_cells)
    least_spot = spots[0]
    most_spot = (spots[0] + 1 + spots[1] % (total_cells - 1)) % total_cells
    flat_cells = jnp.arange(total_cells, dtype=jnp.int32).reshape(NX, NY, NZ)
    values = jnp.where(flat_cells == least_spot, least_value, values)
    values = jnp.where(flat_cells == most_spot, most_value, values)
    return values


def touch_ends(result, own_key, least, largest):
    index_at = [jax.random.randint(jax.random.fold_in(own_key, axis), (), 0, length) for axis, length in enumerate(result.shape)]
    widest = result.shape.index(max(result.shape))
    beside = index_at[:widest] + [(index_at[widest] + 1) % result.shape[widest]] + index_at[widest + 1:]
    return result.at[tuple(index_at)].set(least).at[tuple(beside)].set(largest)


def level_of(rng, shape, shards, low, top_value):
    gain = 1.0
    for axis_at, shards_of in shards:
        draws = jax.random.uniform(jax.random.fold_in(jax.random.fold_in(rng, 6), axis_at), (shards_of,), jnp.float32, low / len(shards), top_value / len(shards))
        gain = gain * jnp.repeat(jnp.exp(draws), shape[axis_at] // shards_of).reshape((-1,) + (1,) * (len(shape) - 1 - axis_at))
    return gain


def scatter_about(own_key, dims, deviation, reach, pieces=(), held_as=jnp.bfloat16):
    result = deviation * jax.random.normal(own_key, dims, jnp.float32)
    if pieces:
        result = result * level_of(own_key, dims, pieces, -0.22, 0.18)
    return jnp.clip(result, -reach, reach).astype(held_as)


def setup_inputs(seed: int = 0, part: int = 0) -> dict:
    keys = jax.random.split(jax.random.key(seed), 6)
    own_keys = jax.random.split(jax.random.fold_in(keys[5], part), 6)
    conductivity = draw_conductivity(jax.random.fold_in(jax.random.fold_in(keys[5], part), 71), part)
    source_field = scatter_about(own_keys[1], (3, NX, NY, NZ), 1.0, 6.0, ((1, 8),), jnp.float32)
    shifts = jnp.clip(jnp.exp(jax.random.uniform(keys[2], (POLES,), jnp.float32, math.log(1.0), math.log(10.0))), 1.0, 10.0)
    residues = scatter_about(keys[3], (GATES, POLES), 1.0, 4.0, (), jnp.float32)
    receivers = touch_ends(jax.random.randint(own_keys[4], (REC,), 0, NX * NY * NZ), jax.random.fold_in(own_keys[4], 1), 0, (NX * NY * NZ) - 1).astype(jnp.int32)
    return {"conductivity": conductivity, "source_field": source_field, "shifts": shifts, "residues": residues, "receivers": receivers}


def forward(values, which_axis):
    target = which_axis % values.ndim
    widths = [(0, 0)] * values.ndim
    widths[target] = (0, 1)
    padded = jnp.pad(values, widths)
    return lax.slice_in_dim(padded, 1, padded.shape[target], axis=target) - values


def backward(values, which_axis):
    target = which_axis % values.ndim
    widths = [(0, 0)] * values.ndim
    widths[target] = (1, 0)
    padded = jnp.pad(values, widths)
    return lax.slice_in_dim(padded, 0, values.shape[target], axis=target) - values


def curl_curl(padded_field):
    comp_x = padded_field[..., 0, :, :, :]
    comp_y = padded_field[..., 1, :, :, :]
    comp_z = padded_field[..., 2, :, :, :]
    face_x = forward(comp_z, -2) - forward(comp_y, -1)
    face_y = forward(comp_x, -1) - forward(comp_z, -3)
    face_z = forward(comp_y, -3) - forward(comp_x, -2)
    edge_x = backward(face_y, -1) - backward(face_z, -2)
    edge_y = backward(face_z, -3) - backward(face_x, -1)
    edge_z = backward(face_x, -2) - backward(face_y, -3)
    return jnp.stack([edge_x, edge_y, edge_z], axis=-4)


def operate(direction, conductivity, shift_value):
    padded = jnp.pad(direction, ((0, 0), (1, 1), (1, 1), (1, 1)))
    inner = curl_curl(padded)[:, 1:-1, 1:-1, 1:-1]
    return inner + shift_value * conductivity * direction


def reference(conductivity, source_field, shifts, residues, receivers):
    lower = jnp.min(conductivity)
    upper = jnp.max(conductivity)
    rhs = conductivity * source_field
    gated = jnp.zeros((GATES,) + source_field.shape, jnp.float32)
    for pole_index in range(POLES):
        shift_value = shifts[pole_index]
        low_end = shift_value * lower
        high_end = 16.0 + shift_value * upper
        center = (high_end + low_end) / 2.0
        spread = (high_end - low_end) / 2.0
        scaled = center / spread
        residual = rhs
        direction = rhs / center
        ratio_old = 1.0 / scaled
        solution = direction
        for turn_index in range(ITERS):
            residual = residual - operate(direction, conductivity, shift_value)
            ratio_new = 1.0 / (2.0 * scaled - ratio_old)
            direction = ratio_new * ratio_old * direction + (2.0 * ratio_new / spread) * residual
            ratio_old = ratio_new
            solution = solution + direction
        gated = gated + residues[:, pole_index].reshape(-1, 1, 1, 1, 1) * solution[None]
    traces = gated.reshape(GATES, 3, -1)[:, :, receivers]
    return gated, traces
```

```python
import functools

import jax
import jax.numpy as jnp
from jax import lax
from jax.experimental import pallas as pl
from jax.experimental.pallas import tpu as pltpu
from jax.sharding import PartitionSpec as P

MID = 4.65
WORDS = 10
SLOTS = 32
TILE = 8
VMEM = pl.BlockSpec(memory_space=pltpu.VMEM)
SMEM = pl.BlockSpec(memory_space=pltpu.SMEM)
PARAMS = pltpu.CompilerParams(vmem_limit_bytes=48 * 1024 * 1024)


def sub_next(v):
    return pltpu.roll(v, v.shape[0] - 1, 0)


def sub_prev(v):
    return pltpu.roll(v, 1, 0)


def lanes_of(v):
    return lax.broadcasted_iota(jnp.int32, v.shape, 1)


def rows_of(v):
    return lax.broadcasted_iota(jnp.int32, v.shape, 0)


def lane_next(v):
    return jnp.where(lanes_of(v) == v.shape[1] - 1, 0.0, pltpu.roll(v, v.shape[1] - 1, 1))


def lane_prev(v, first):
    return jnp.where(lanes_of(v) == 0, first, pltpu.roll(v, 1, 1))


def part_keep(core):
    row = lax.broadcasted_iota(jnp.int32, (TILE, 128), 0)
    return jnp.where(core == 0, (row < 5).astype(jnp.float32), (row >= 5).astype(jnp.float32))


def own_rows(half, core):
    return pl.ds(pl.multiple_of(core * half, TILE), half)


def extra_rows(half, core):
    return pl.ds(pl.multiple_of(half - core * TILE, TILE), TILE)


def to_front(tile, core):
    return jnp.where(core == 0, tile, pltpu.roll(tile, 3, 0))


def from_front(tile, core):
    tile = jnp.where(rows_of(tile) < 3, tile, 0.0)
    return jnp.where(core == 0, tile, pltpu.roll(tile, TILE - 3, 0))


def pack_extras(near, far, ends):
    row = rows_of(ends)
    spare = [
        pltpu.roll(far[0], 6, 0),
        pltpu.roll(far[1], 6, 0),
        jnp.where(row == 6, pltpu.roll(far[0], 4, 0), pltpu.roll(far[1], 5, 0)),
        pltpu.roll(ends, 6, 0),
    ]
    return [
        jnp.where(
            row < 3,
            near[2 * at],
            jnp.where(row < 6, pltpu.roll(near[2 * at + 1], 3, 0), spare[at]),
        )
        for at in range(4)
    ]


def unpack_near(tiles, at, core):
    tile = tiles[at // 2]
    return from_front(pltpu.roll(tile, TILE - 3, 0) if at % 2 else tile, core)


def unpack_far(tiles, at, core):
    last = pltpu.roll(tiles[2], 4 - at, 0)
    return from_front(jnp.where(rows_of(last) < 2, pltpu.roll(tiles[at], 2, 0), last), core)


def extremes(cond_ref):
    top = jnp.max(cond_ref[...], axis=0)
    low = jnp.max(-cond_ref[...], axis=0)
    return jnp.max(top, axis=0, keepdims=True), jnp.max(low, axis=0, keepdims=True)


def send_kernel(cond_ref, src_ref, first_ref, second_ref):
    core = lax.axis_index("pole")
    odd = lax.rem(lax.axis_index("space"), 2)
    layers, rows, _ = cond_ref.shape
    half = rows // 2
    own, extra = own_rows(half, core), extra_rows(half, core)
    keep = part_keep(core)

    def load(layer):
        cond = jnp.concatenate([cond_ref[layer, own, :], cond_ref[layer, extra, :] * keep], axis=0)
        return cond, [
            cond * jnp.concatenate([src_ref[c, layer, own, :], src_ref[c, layer, extra, :]], axis=0)
            for c in range(3)
        ]

    top, low = extremes(cond_ref)
    row = lax.broadcasted_iota(jnp.int32, (TILE, 128), 0)
    ends = jnp.where(row == 0, top, low)
    for upward in (True, False):
        near = []
        for distance in (1, 2):
            cond, field = load(layers - distance if upward else distance - 1)
            near.append((cond, field))
        cond, (fx, fy, fz) = load(layers - 3 if upward else 2)
        far = [fy + sub_next(fx) - fx, fz + lane_next(fx) - fx] if upward else [fy, fz]
        blocks = [*near[0][1], near[0][0], *near[1][1], near[1][0], *far]
        edges = [to_front(block[half:], core) for block in blocks]
        pairs = pack_extras(edges[:8], edges[8:], ends)

        def write(out_ref):
            for at, block in enumerate(blocks):
                out_ref[at * half : (at + 1) * half, :] = block[:half]
            base = len(blocks) * half
            for at, pair in enumerate(pairs):
                out_ref[base + at * TILE : base + (at + 1) * TILE, :] = pair

        with_first = odd == 0 if upward else odd == 1

        @pl.when(with_first)
        def _():
            write(first_ref)

        @pl.when(jnp.logical_not(with_first))
        def _():
            write(second_ref)


def list_kernel(rec_ref, list_ref, count_ref, *, layers, rows, depth):
    core = lax.axis_index("pole")
    base = lax.axis_index("space") * layers
    half = rows // 2

    def step(at, count):
        cell = rec_ref[at]
        x = lax.div(cell, rows * depth) - base
        y = lax.rem(lax.div(cell, depth), rows) - core * half
        owned = (x >= 0) & (x < layers) & (y >= 0) & (y < half)
        list_ref[count] = at
        return count + owned.astype(jnp.int32)

    count_ref[0] = lax.fori_loop(0, rec_ref.shape[0], step, jnp.int32(0))


def curl_curl(get_u, get, layers, put, half, trimmed=False):
    first = layers[0]
    u_y, u_z = get_u(first - 1)
    _, g, e = get(first, (1, 2))
    prev_z, prev_y = g - u_y, u_z - e
    for layer in layers:
        f, g, e = get(layer, (0, 1, 2))
        _, g_up, e_up = get(layer + 1, (1, 2))
        h_z = g_up - (g + (sub_next(f) - f))
        h_y = (e + (lane_next(f) - f)) - e_up
        h_x = (sub_next(e) - e) - (lane_next(g) - g)
        out_x = (h_z - sub_prev(h_z)) + (lane_prev(h_y, f) - h_y) - 8.0 * f
        out_y = (h_x - lane_prev(h_x, -g)) + (prev_z - h_z) - 8.0 * g
        out_z = (h_y - prev_y) + (sub_prev(h_x) - h_x) - 8.0 * e
        prev_z, prev_y = h_z, h_y
        put(layer, (out_x, out_y, out_z))


def basis_kernel(
    cond_ref, src_ref, first_ref, second_ref, rec_ref, list_ref, count_ref,
    bas_ref, sel_ref,
    sig, low3, high3, t00, t10, t11, t20, t21, t22,
):
    core = lax.axis_index("pole")
    place = lax.axis_index("space")
    odd = lax.rem(place, 2)
    layers, rows, depth = cond_ref.shape
    half = rows // 2
    own, extra = own_rows(half, core), extra_rows(half, core)
    keep = part_keep(core)
    low_ok = (place > 0).astype(jnp.float32)
    high_ok = (place < lax.axis_size("space") - 1).astype(jnp.float32)

    def received(upward, at):
        part = pl.ds(at * half, half)
        from_first = odd == 1 if upward else odd == 0
        return jnp.where(from_first, first_ref[part, :], second_ref[part, :])

    def received_tile(upward, at):
        part = pl.ds(10 * half + at * TILE, TILE)
        from_first = odd == 1 if upward else odd == 0
        return jnp.where(from_first, first_ref[part, :], second_ref[part, :])

    for layer in range(layers):
        cond = jnp.concatenate([cond_ref[layer, own, :], cond_ref[layer, extra, :] * keep], axis=0)
        moved = cond - MID
        sig[layer + 2] = moved
        for c in range(3):
            field = cond * jnp.concatenate(
                [src_ref[c, layer, own, :], src_ref[c, layer, extra, :]], axis=0
            )
            t00[layer + 2, c] = field
            t11[layer + 2, c] = moved * field
    for upward in (True, False):
        tiles = [received_tile(upward, at) for at in range(4)]
        for distance in (1, 2):
            slot = 2 - distance if upward else layers + 1 + distance
            base = (distance - 1) * 4
            moved = jnp.concatenate(
                [received(upward, base + 3), unpack_near(tiles, base + 3, core)], axis=0
            ) - MID
            sig[slot] = moved
            for c in range(3):
                field = jnp.concatenate(
                    [received(upward, base + c), unpack_near(tiles, base + c, core)], axis=0
                )
                t00[slot, c] = field
                t11[slot, c] = moved * field
        far = low3 if upward else high3
        for at in range(2):
            far[at] = jnp.concatenate(
                [received(upward, 8 + at), unpack_far(tiles, at, core)], axis=0
            )

    def sums(ref):
        def get_u(slot):
            f, g, e = ref[slot, 0], ref[slot, 1], ref[slot, 2]
            return g + (sub_next(f) - f), e + (lane_next(f) - f)

        return get_u

    def reader(ref):
        def get(slot, which):
            return [ref[slot, c] if c in which else None for c in range(3)]

        return get

    def inside(slot, value):
        value = jnp.concatenate([value[:half], value[half:] * keep], axis=0)
        if slot < 2:
            return value * low_ok
        if slot > layers + 1:
            return value * high_ok
        return value

    def get_b(slot, which):
        if slot > layers + 3:
            return None, high3[0], high3[1]
        return [t00[slot, c] if c in which else None for c in range(3)]

    def put_10(slot, out):
        for c in range(3):
            t10[slot, c] = inside(slot, out[c])

    curl_curl(lambda slot: (low3[0], low3[1]), get_b, list(range(layers + 4)), put_10, half)

    def put_20(slot, out):
        for c in range(3):
            t20[slot, c] = inside(slot, out[c])

    def put_21(slot, out):
        for c in range(3):
            t21[slot, c] = inside(slot, out[c]) + sig[slot] * t10[slot, c]
            t22[slot, c] = sig[slot] * t11[slot, c]

    middle = list(range(1, layers + 3))
    curl_curl(sums(t10), reader(t10), middle, put_20, half)
    curl_curl(sums(t11), reader(t11), middle, put_21, half)

    def store(word, slot, c, value):
        base = ((slot - 2) * SLOTS + word * 3 + c) * half
        bas_ref[base : base + half, :] = value

    inner = list(range(2, layers + 2))
    for slot in inner:
        for c in range(3):
            for word, ref in enumerate((t00, t10, t11, t20, t21, t22)):
                store(word, slot, c, ref[slot, c, :half, :])
            store(9, slot, c, sig[slot, :half, :] * t22[slot, c, :half, :])
        for spare in range(WORDS * 3, SLOTS):
            base = ((slot - 2) * SLOTS + spare) * half
            bas_ref[base : base + half, :] = jnp.zeros((half, depth), jnp.float32)

    def put_3(word, before):
        def put(slot, out):
            for c in range(3):
                value = out[c][:half]
                if before is not None:
                    value = value + sig[slot, :half, :] * before[slot, c, :half, :]
                store(word, slot, c, value)

        return put

    curl_curl(sums(t20), reader(t20), inner, put_3(6, None), half)
    curl_curl(sums(t21), reader(t21), inner, put_3(7, t20), half)
    curl_curl(sums(t22), reader(t22), inner, put_3(8, t21), half)

    groups = sel_ref.shape[0]
    for group in range(groups):
        sel_ref[group, :SLOTS, :] = jnp.zeros((SLOTS, depth), jnp.float32)
    top, low = extremes(cond_ref)
    tile = first_ref[10 * half + 3 * TILE : 10 * half + 4 * TILE, :]
    row = lax.broadcasted_iota(jnp.int32, (TILE, 128), 0)
    ends = jnp.maximum(jnp.where(row == 0, top, low), jnp.where(row == 0, tile[6:7], tile[7:8]))
    for group in range(groups):
        sel_ref[group, SLOTS:, :] = ends

    lane = lax.broadcasted_iota(jnp.int32, (SLOTS, depth), 1)

    def pick(at, carry):
        which = list_ref[at]
        cell = rec_ref[which]
        x = lax.div(cell, rows * depth) - place * layers
        y = lax.rem(lax.div(cell, depth), rows) - core * half
        z = lax.rem(cell, depth)
        block = bas_ref[pl.ds(x * (SLOTS * half) + y, SLOTS, stride=half), :]
        target = lax.rem(which, 128)
        group = lax.div(which, 128)
        block = pltpu.roll(block, lax.rem(target - z + 128, 128), 1)
        sel_ref[group, :SLOTS, :] = jnp.where(lane == target, block, sel_ref[group, :SLOTS, :])
        return carry

    lax.fori_loop(0, count_ref[0], pick, 0)


def weights(ends_ref, shifts_ref, res_ref, out_ref):
    upper = jnp.max(ends_ref[0, SLOTS : SLOTS + 1, :], axis=1, keepdims=True)
    lower = -jnp.max(ends_ref[0, SLOTS + 1 : SLOTS + 2, :], axis=1, keepdims=True)
    shift = shifts_ref[...]
    low_end = shift * lower
    high_end = 16.0 + shift * upper
    center = (high_end + low_end) / 2.0
    spread = (high_end - low_end) / 2.0
    scaled = center / spread
    residual = [jnp.ones_like(shift)]
    direction = [1.0 / center]
    ratio = 1.0 / scaled
    total = list(direction)
    for _ in range(3):
        applied = [center * d for d in direction] + [jnp.zeros_like(shift)]
        for at, d in enumerate(direction):
            applied[at + 1] = applied[at + 1] + spread * d
        residual = [
            (residual[at] if at < len(residual) else 0.0) - a for at, a in enumerate(applied)
        ]
        ratio_new = 1.0 / (2.0 * scaled - ratio)
        grown = [(2.0 * ratio_new / spread) * r for r in residual]
        direction = [
            g + ratio_new * ratio * direction[at] if at < len(direction) else g
            for at, g in enumerate(grown)
        ]
        ratio = ratio_new
        total = [
            d + total[at] if at < len(total) else d for at, d in enumerate(direction)
        ]
    offset = shift * (MID - (upper + lower) / 2.0)
    inverse = 1.0 / spread
    y0, y1, y2, y3 = total
    y1 = y1 * inverse
    y2 = y2 * inverse * inverse
    y3 = y3 * inverse * inverse * inverse
    powers = [
        y0 + offset * (y1 + offset * (y2 + offset * y3)),
        y1 + offset * (2.0 * y2 + 3.0 * offset * y3),
        y2 + 3.0 * offset * y3,
        y3,
    ]
    word = 0
    res = res_ref[...]
    for m in range(4):
        term = powers[m]
        for _ in range(m + 1):
            column = jnp.sum(res * term, axis=1, keepdims=True)
            out_ref[word, : res.shape[0], :] = jnp.broadcast_to(column, (res.shape[0], 128))
            term = term * shift
            word += 1


def combine(w_ref, bas_ref, out_ref, gates):
    half = bas_ref.shape[2]
    for c in range(3):
        for top in range(0, half, TILE):
            terms = [bas_ref[0, word * 3 + c, top : top + TILE, :] for word in range(WORDS)]
            for g in range(gates):
                total = w_ref[0, g : g + 1, :] * terms[0]
                for word in range(1, WORDS):
                    total = total + w_ref[word, g : g + 1, :] * terms[word]
                out_ref[g, c, 0, top : top + TILE, :] = total


def gate_kernel(ends_ref, shifts_ref, res_ref, bas_ref, out_ref, w_ref):
    @pl.when(pl.program_id(0) == 0)
    def _():
        weights(ends_ref, shifts_ref, res_ref, w_ref)

    combine(w_ref, bas_ref, out_ref, res_ref.shape[0])


def trace_kernel(w_ref, sel_ref, out_ref):
    gates = out_ref.shape[0]
    for group in range(sel_ref.shape[0]):
        for c in range(3):
            total = None
            for word in range(WORDS):
                at = word * 3 + c
                term = w_ref[word, :gates, :] * sel_ref[group, at : at + 1, :]
                total = term if total is None else total + term
            for g in range(gates):
                out_ref[g, c : c + 1, group * 128 : (group + 1) * 128] = total[g : g + 1]


def per_device(conductivity, source_field, shifts, residues, receivers):
    layers, rows, depth = conductivity.shape
    half = rows // 2
    gates, poles = residues.shape
    count = receivers.shape[0]
    groups = count // 128
    size = lax.axis_size("space")
    f32 = jnp.float32
    message = jax.ShapeDtypeStruct((10 * half + 4 * TILE, depth), f32)

    first, second = pl.pallas_call(
        send_kernel,
        out_shape=[message, message],
        in_specs=[VMEM, VMEM],
        out_specs=[VMEM, VMEM],
        compiler_params=PARAMS,
        name="send",
    )(conductivity, source_field)
    far_pairs = [(i, i + 1) for i in range(1, size - 1, 2)]
    far_pairs = far_pairs + [(j, i) for i, j in far_pairs]
    second = lax.ppermute(second, "space", far_pairs)
    first = lax.ppermute(first, "space", [(i, i ^ 1) for i in range(size)])

    listed, owned = pl.pallas_call(
        functools.partial(list_kernel, layers=layers, rows=rows, depth=depth),
        out_shape=[jax.ShapeDtypeStruct((count,), jnp.int32), jax.ShapeDtypeStruct((1,), jnp.int32)],
        in_specs=[SMEM],
        out_specs=[SMEM, SMEM],
        name="owned",
    )(receivers)

    def field(slots):
        return pltpu.VMEM((slots, 3, half + TILE, depth), f32)

    basis, sel = pl.pallas_call(
        basis_kernel,
        out_shape=[
            jax.ShapeDtypeStruct((layers * SLOTS * half, depth), f32),
            jax.ShapeDtypeStruct((groups, SLOTS + TILE, 128), f32),
        ],
        in_specs=[VMEM, VMEM, VMEM, VMEM, SMEM, SMEM, SMEM],
        out_specs=[VMEM, VMEM],
        scratch_shapes=[
            pltpu.VMEM((layers + 4, half + TILE, depth), f32),
            pltpu.VMEM((2, half + TILE, depth), f32),
            pltpu.VMEM((2, half + TILE, depth), f32),
            *[field(layers + 4) for _ in range(6)],
        ],
        compiler_params=PARAMS,
        name="basis",
    )(conductivity, source_field, first, second, receivers, listed, owned)

    is_end = lax.broadcasted_iota(jnp.int32, sel.shape, 1) >= SLOTS
    stride = 2
    while stride < size:
        other = lax.ppermute(sel, "space", [(i, i ^ stride) for i in range(size)])
        sel = jnp.where(is_end, jnp.maximum(sel, other), sel + other)
        stride *= 2
    ends = sel
    sel = sel[:, :SLOTS]
    sel = sel + lax.ppermute(sel, "space", [(i, i ^ 1) for i in range(size)])
    sel = sel + lax.ppermute(sel, "pole", [(0, 1), (1, 0)])

    gated, w = pl.pallas_call(
        gate_kernel,
        grid=(layers,),
        out_shape=[
            jax.ShapeDtypeStruct((gates, 3, layers, half, depth), f32),
            jax.ShapeDtypeStruct((WORDS, 16, 128), f32),
        ],
        in_specs=[
            pl.BlockSpec(ends.shape, lambda i: (0, 0, 0)),
            pl.BlockSpec((1, poles), lambda i: (0, 0)),
            pl.BlockSpec((gates, poles), lambda i: (0, 0)),
            pl.BlockSpec((1, SLOTS, half, depth), lambda i: (i, 0, 0, 0)),
        ],
        out_specs=[
            pl.BlockSpec((gates, 3, 1, half, depth), lambda i: (0, 0, i, 0, 0)),
            pl.BlockSpec((WORDS, 16, 128), lambda i: (0, 0, 0)),
        ],
        compiler_params=PARAMS,
        name="gates",
    )(ends, shifts.reshape(1, poles), residues, basis.reshape(layers, SLOTS, half, depth))

    traces = pl.pallas_call(
        trace_kernel,
        out_shape=jax.ShapeDtypeStruct((gates, 3, count), f32),
        in_specs=[VMEM, VMEM],
        out_specs=VMEM,
        compiler_params=PARAMS,
        name="traces",
    )(w, sel)
    return gated, traces


def solution(mesh):
    placed = (
        P(("survey", "space"), None, None),
        P(None, ("survey", "space"), None, None),
        P(),
        P(),
        P("survey"),
    )
    return jax.shard_map(
        per_device,
        mesh=mesh,
        in_specs=placed,
        out_specs=(P(None, None, ("survey", "space"), "pole", None), P(None, None, "survey")),
        check_vma=False,
    )
```

```python
import functools

import jax
import jax.numpy as jnp
from jax import lax
from jax.experimental import pallas as pl
from jax.experimental.pallas import tpu as pltpu
from jax.sharding import PartitionSpec as P

MID = 4.65
WORDS = 10
SLOTS = 32
TILE = 8
VMEM = pl.BlockSpec(memory_space=pltpu.VMEM)
SMEM = pl.BlockSpec(memory_space=pltpu.SMEM)
PARAMS = pltpu.CompilerParams(vmem_limit_bytes=48 * 1024 * 1024)


def sub_next(v):
    return pltpu.roll(v, v.shape[0] - 1, 0)


def sub_prev(v):
    return pltpu.roll(v, 1, 0)


def lanes_of(v):
    return lax.broadcasted_iota(jnp.int32, v.shape, 1)


def rows_of(v):
    return lax.broadcasted_iota(jnp.int32, v.shape, 0)


def lane_next(v):
    return jnp.where(lanes_of(v) == v.shape[1] - 1, 0.0, pltpu.roll(v, v.shape[1] - 1, 1))


def lane_prev(v, first):
    return jnp.where(lanes_of(v) == 0, first, pltpu.roll(v, 1, 1))


def part_keep(core):
    row = lax.broadcasted_iota(jnp.int32, (TILE, 128), 0)
    return jnp.where(core == 0, (row < 5).astype(jnp.float32), (row >= 5).astype(jnp.float32))


def own_rows(half, core):
    return pl.ds(pl.multiple_of(core * half, TILE), half)


def extra_rows(half, core):
    return pl.ds(pl.multiple_of(half - core * TILE, TILE), TILE)


def to_front(tile, core):
    return jnp.where(core == 0, tile, pltpu.roll(tile, 3, 0))


def from_front(tile, core):
    tile = jnp.where(rows_of(tile) < 3, tile, 0.0)
    return jnp.where(core == 0, tile, pltpu.roll(tile, TILE - 3, 0))


def pack_extras(near, far, ends):
    row = rows_of(ends)
    spare = [
        pltpu.roll(far[0], 6, 0),
        pltpu.roll(far[1], 6, 0),
        jnp.where(row == 6, pltpu.roll(far[0], 4, 0), pltpu.roll(far[1], 5, 0)),
        pltpu.roll(ends, 6, 0),
    ]
    return [
        jnp.where(
            row < 3,
            near[2 * at],
            jnp.where(row < 6, pltpu.roll(near[2 * at + 1], 3, 0), spare[at]),
        )
        for at in range(4)
    ]


def unpack_near(tiles, at, core):
    tile = tiles[at // 2]
    return from_front(pltpu.roll(tile, TILE - 3, 0) if at % 2 else tile, core)


def unpack_far(tiles, at, core):
    last = pltpu.roll(tiles[2], 4 - at, 0)
    return from_front(jnp.where(rows_of(last) < 2, pltpu.roll(tiles[at], 2, 0), last), core)


def send_kernel(cond_hbm, src_hbm, first_ref, second_ref, cond_out, field_out, ends_ref, cond_ref, src_ref, sems):
    core = lax.axis_index("pole")
    odd = lax.rem(lax.axis_index("space"), 2)
    layers, rows, _ = cond_ref.shape
    half = rows // 2
    own, extra = own_rows(half, core), extra_rows(half, core)
    keep = part_keep(core)
    copies = [pltpu.make_async_copy(cond_hbm, cond_ref, sems.at[0])] + [
        pltpu.make_async_copy(src_hbm.at[c], src_ref.at[c], sems.at[1 + c]) for c in range(3)
    ]
    for copy in copies:
        copy.start()
    for copy in copies:
        copy.wait()

    conds, fields = [], []
    for layer in range(layers):
        cond = jnp.concatenate([cond_ref[layer, own, :], cond_ref[layer, extra, :] * keep], axis=0)
        field = [
            cond * jnp.concatenate([src_ref[c, layer, own, :], src_ref[c, layer, extra, :]], axis=0)
            for c in range(3)
        ]
        cond_out[layer] = cond
        for c in range(3):
            field_out[layer, c] = field[c]
        conds.append(cond)
        fields.append(field)

    top = jnp.max(jnp.max(cond_ref[...], axis=0), axis=0, keepdims=True)
    low = jnp.max(-jnp.min(cond_ref[...], axis=0), axis=0, keepdims=True)
    row = lax.broadcasted_iota(jnp.int32, (TILE, 128), 0)
    ends = jnp.where(row == 0, top, low)
    ends_ref[...] = ends
    for upward in (True, False):
        near = [layers - 1, layers - 2] if upward else [0, 1]
        fx, fy, fz = fields[layers - 3 if upward else 2]
        far = [fy + sub_next(fx) - fx, fz + lane_next(fx) - fx] if upward else [fy, fz]
        blocks = [v for layer in near for v in (*fields[layer], conds[layer])] + far
        edges = [to_front(block[half:], core) for block in blocks]
        pairs = pack_extras(edges[:8], edges[8:], ends)

        def write(out_ref):
            for at, block in enumerate(blocks):
                out_ref[at * half : (at + 1) * half, :] = block[:half]
            base = len(blocks) * half
            for at, pair in enumerate(pairs):
                out_ref[base + at * TILE : base + (at + 1) * TILE, :] = pair

        with_first = odd == 0 if upward else odd == 1

        @pl.when(with_first)
        def _():
            write(first_ref)

        @pl.when(jnp.logical_not(with_first))
        def _():
            write(second_ref)


def list_kernel(rec_ref, shifts_ref, res_ref, list_ref, par_ref, square, *, layers, rows, depth):
    core = lax.axis_index("pole")
    base = lax.axis_index("space") * layers
    half = rows // 2
    total = rec_ref.shape[0]

    def step(at, count):
        cell = rec_ref[at]
        x = lax.div(cell, rows * depth) - base
        y = lax.rem(lax.div(cell, depth), rows) - core * half
        owned = (x >= 0) & (x < layers) & (y >= 0) & (y < half)
        start = x * (SLOTS * half) + y
        list_ref[count] = (start * depth + lax.rem(cell, depth)) * total + at
        return count + owned.astype(jnp.int32)

    list_ref[total] = lax.fori_loop(0, total, step, jnp.int32(0), unroll=8)
    poles, gates = res_ref.shape
    square[...] = jnp.zeros_like(square)
    square[:poles, :gates] = res_ref[...]
    par_ref[...] = jnp.zeros_like(par_ref)
    par_ref[TILE : TILE + gates, :poles] = square[...].T[:gates, :poles]
    par_ref[:1, :poles] = shifts_ref[...]


def curl_curl(get_u, get, layers, put, half, trimmed=False):
    first = layers[0]
    u_y, u_z = get_u(first - 1)
    _, g, e = get(first, (1, 2))
    prev_z, prev_y = g - u_y, u_z - e
    for layer in layers:
        f, g, e = get(layer, (0, 1, 2))
        _, g_up, e_up = get(layer + 1, (1, 2))
        h_z = g_up - (g + (sub_next(f) - f))
        h_y = (e + (lane_next(f) - f)) - e_up
        h_x = (sub_next(e) - e) - (lane_next(g) - g)
        out_x = (h_z - sub_prev(h_z)) + (lane_prev(h_y, f) - h_y) - 8.0 * f
        out_y = (h_x - lane_prev(h_x, -g)) + (prev_z - h_z) - 8.0 * g
        out_z = (h_y - prev_y) + (sub_prev(h_x) - h_x) - 8.0 * e
        prev_z, prev_y = h_z, h_y
        put(layer, (out_x, out_y, out_z))


def basis_kernel(
    cond_ref, field_ref, ends_ref, first_ref, second_ref, list_hbm,
    bas_ref, sel_ref,
    sig, low3, high3, t00, t10, t11, t20, t21, t22, list_ref, list_sem,
):
    core = lax.axis_index("pole")
    place = lax.axis_index("space")
    odd = lax.rem(place, 2)
    layers, reach, depth = cond_ref.shape
    half = reach - TILE
    keep = part_keep(core)
    list_copy = pltpu.make_async_copy(list_hbm, list_ref, list_sem)
    list_copy.start()
    low_ok = (place > 0).astype(jnp.float32)
    high_ok = (place < lax.axis_size("space") - 1).astype(jnp.float32)

    def received(upward, at):
        part = pl.ds(at * half, half)
        from_first = odd == 1 if upward else odd == 0
        return jnp.where(from_first, first_ref[part, :], second_ref[part, :])

    def received_tile(upward, at):
        part = pl.ds(10 * half + at * TILE, TILE)
        from_first = odd == 1 if upward else odd == 0
        return jnp.where(from_first, first_ref[part, :], second_ref[part, :])

    for layer in range(layers):
        moved = cond_ref[layer] - MID
        sig[layer + 2] = moved
        for c in range(3):
            field = field_ref[layer, c]
            t00[layer + 2, c] = field
            t11[layer + 2, c] = moved * field
    for upward in (True, False):
        tiles = [received_tile(upward, at) for at in range(4)]
        for distance in (1, 2):
            slot = 2 - distance if upward else layers + 1 + distance
            base = (distance - 1) * 4
            moved = jnp.concatenate(
                [received(upward, base + 3), unpack_near(tiles, base + 3, core)], axis=0
            ) - MID
            sig[slot] = moved
            for c in range(3):
                field = jnp.concatenate(
                    [received(upward, base + c), unpack_near(tiles, base + c, core)], axis=0
                )
                t00[slot, c] = field
                t11[slot, c] = moved * field
        far = low3 if upward else high3
        for at in range(2):
            far[at] = jnp.concatenate(
                [received(upward, 8 + at), unpack_far(tiles, at, core)], axis=0
            )

    def sums(ref):
        def get_u(slot):
            f, g, e = ref[slot, 0], ref[slot, 1], ref[slot, 2]
            return g + (sub_next(f) - f), e + (lane_next(f) - f)

        return get_u

    def reader(ref):
        def get(slot, which):
            return [ref[slot, c] if c in which else None for c in range(3)]

        return get

    def inside(slot, value):
        value = jnp.concatenate([value[:half], value[half:] * keep], axis=0)
        if slot < 2:
            return value * low_ok
        if slot > layers + 1:
            return value * high_ok
        return value

    def get_b(slot, which):
        if slot > layers + 3:
            return None, high3[0], high3[1]
        return [t00[slot, c] if c in which else None for c in range(3)]

    def put_10(slot, out):
        for c in range(3):
            t10[slot, c] = inside(slot, out[c])

    curl_curl(lambda slot: (low3[0], low3[1]), get_b, list(range(layers + 4)), put_10, half)

    def put_20(slot, out):
        for c in range(3):
            t20[slot, c] = inside(slot, out[c])

    def put_21(slot, out):
        for c in range(3):
            t21[slot, c] = inside(slot, out[c]) + sig[slot] * t10[slot, c]
            t22[slot, c] = sig[slot] * t11[slot, c]

    middle = list(range(1, layers + 3))
    curl_curl(sums(t10), reader(t10), middle, put_20, half)
    curl_curl(sums(t11), reader(t11), middle, put_21, half)

    def store(word, slot, c, value):
        base = ((slot - 2) * SLOTS + word * 3 + c) * half
        bas_ref[base : base + half, :] = value

    inner = list(range(2, layers + 2))
    for slot in inner:
        for c in range(3):
            for word, ref in enumerate((t00, t10, t11, t20, t21, t22)):
                store(word, slot, c, ref[slot, c, :half, :])
            store(9, slot, c, sig[slot, :half, :] * t22[slot, c, :half, :])
        for spare in range(WORDS * 3, SLOTS):
            base = ((slot - 2) * SLOTS + spare) * half
            bas_ref[base : base + half, :] = jnp.zeros((half, depth), jnp.float32)

    def put_3(word, before):
        def put(slot, out):
            for c in range(3):
                value = out[c][:half]
                if before is not None:
                    value = value + sig[slot, :half, :] * before[slot, c, :half, :]
                store(word, slot, c, value)

        return put

    curl_curl(sums(t20), reader(t20), inner, put_3(6, None), half)
    curl_curl(sums(t21), reader(t21), inner, put_3(7, t20), half)
    curl_curl(sums(t22), reader(t22), inner, put_3(8, t21), half)

    groups = sel_ref.shape[0]
    for group in range(groups):
        sel_ref[group, :SLOTS, :] = jnp.zeros((SLOTS, depth), jnp.float32)
    tile = first_ref[10 * half + 3 * TILE : 10 * half + 4 * TILE, :]
    row = lax.broadcasted_iota(jnp.int32, (TILE, 128), 0)
    ends = jnp.maximum(ends_ref[...], jnp.where(row == 0, tile[6:7], tile[7:8]))
    for group in range(groups):
        sel_ref[group, SLOTS:, :] = ends

    lane = lax.broadcasted_iota(jnp.int32, (SLOTS, depth), 1)

    total = list_ref.shape[0] - 1
    list_copy.wait()

    def pick(at, carry):
        code = list_ref[at]
        which = lax.rem(code, total)
        cell = lax.div(code, total)
        z = lax.rem(cell, depth)
        block = bas_ref[pl.ds(lax.div(cell, depth), SLOTS, stride=half), :]
        target = lax.rem(which, 128)
        group = lax.div(which, 128)
        block = pltpu.roll(block, lax.rem(target - z + 128, 128), 1)
        sel_ref[group, :SLOTS, :] = jnp.where(lane == target, block, sel_ref[group, :SLOTS, :])
        return carry

    lax.fori_loop(0, list_ref[total], pick, 0)


def weights(ends_ref, par_ref, out_ref, gates, poles):
    upper = jnp.max(ends_ref[0, SLOTS : SLOTS + 1, :], axis=1, keepdims=True)
    lower = -jnp.max(ends_ref[0, SLOTS + 1 : SLOTS + 2, :], axis=1, keepdims=True)
    shift = jnp.where(lax.broadcasted_iota(jnp.int32, (1, 128), 1) < poles, par_ref[:1, :], 1.0)
    low_end = shift * lower
    high_end = 16.0 + shift * upper
    center = (high_end + low_end) / 2.0
    spread = (high_end - low_end) / 2.0
    scaled = center / spread
    residual = [jnp.ones_like(shift)]
    direction = [1.0 / center]
    ratio = 1.0 / scaled
    total = list(direction)
    for _ in range(3):
        applied = [center * d for d in direction] + [jnp.zeros_like(shift)]
        for at, d in enumerate(direction):
            applied[at + 1] = applied[at + 1] + spread * d
        residual = [
            (residual[at] if at < len(residual) else 0.0) - a for at, a in enumerate(applied)
        ]
        ratio_new = 1.0 / (2.0 * scaled - ratio)
        grown = [(2.0 * ratio_new / spread) * r for r in residual]
        direction = [
            g + ratio_new * ratio * direction[at] if at < len(direction) else g
            for at, g in enumerate(grown)
        ]
        ratio = ratio_new
        total = [
            d + total[at] if at < len(total) else d for at, d in enumerate(direction)
        ]
    offset = shift * (MID - (upper + lower) / 2.0)
    inverse = 1.0 / spread
    y0, y1, y2, y3 = total
    y1 = y1 * inverse
    y2 = y2 * inverse * inverse
    y3 = y3 * inverse * inverse * inverse
    powers = [
        y0 + offset * (y1 + offset * (y2 + offset * y3)),
        y1 + offset * (2.0 * y2 + 3.0 * offset * y3),
        y2 + 3.0 * offset * y3,
        y3,
    ]
    word = 0
    res = par_ref[TILE : TILE + gates, :]
    for m in range(4):
        term = powers[m]
        for _ in range(m + 1):
            column = jnp.sum(res * term, axis=1, keepdims=True)
            out_ref[word, : res.shape[0], :] = jnp.broadcast_to(column, (res.shape[0], 128))
            term = term * shift
            word += 1


def combine(w_ref, bas_ref, out_ref, gates):
    half = bas_ref.shape[2]
    for c in range(3):
        for top in range(0, half, TILE):
            terms = [bas_ref[0, word * 3 + c, top : top + TILE, :] for word in range(WORDS)]
            for g in range(gates):
                total = w_ref[0, g : g + 1, :] * terms[0]
                for word in range(1, WORDS):
                    total = total + w_ref[word, g : g + 1, :] * terms[word]
                out_ref[g, c, 0, top : top + TILE, :] = total


def gate_kernel(ends_ref, par_ref, bas_ref, out_ref, w_ref, *, poles):
    gates = out_ref.shape[0]

    @pl.when(pl.program_id(0) == 0)
    def _():
        weights(ends_ref, par_ref, w_ref, gates, poles)

    combine(w_ref, bas_ref, out_ref, gates)


def rest_kernel(w_ref, bas_ref, before_ref, out_ref):
    del before_ref
    combine(w_ref, bas_ref, out_ref, out_ref.shape[0])


def trace_kernel(w_ref, sel_ref, out_ref):
    gates = out_ref.shape[0]
    for group in range(sel_ref.shape[0]):
        for c in range(3):
            total = None
            for word in range(WORDS):
                at = word * 3 + c
                term = w_ref[word, :gates, :] * sel_ref[group, at : at + 1, :]
                total = term if total is None else total + term
            for g in range(gates):
                out_ref[g, c : c + 1, group * 128 : (group + 1) * 128] = total[g : g + 1]


def per_device(conductivity, source_field, shifts, residues, receivers):
    layers, rows, depth = conductivity.shape
    half = rows // 2
    gates, poles = residues.shape
    count = receivers.shape[0]
    groups = count // 128
    size = lax.axis_size("space")
    f32 = jnp.float32
    message = jax.ShapeDtypeStruct((10 * half + 4 * TILE, depth), f32)
    hbm = pl.BlockSpec(memory_space=pltpu.HBM)

    first, second, own_cond, own_field, own_ends = pl.pallas_call(
        send_kernel,
        out_shape=[
            message,
            message,
            jax.ShapeDtypeStruct((layers, half + TILE, depth), f32),
            jax.ShapeDtypeStruct((layers, 3, half + TILE, depth), f32),
            jax.ShapeDtypeStruct((TILE, 128), f32),
        ],
        in_specs=[hbm, hbm],
        out_specs=[VMEM] * 5,
        scratch_shapes=[
            pltpu.VMEM((layers, rows, depth), f32),
            pltpu.VMEM((3, layers, rows, depth), f32),
            pltpu.SemaphoreType.DMA((4,)),
        ],
        compiler_params=PARAMS,
        name="send",
    )(conductivity, source_field)
    far_pairs = [(i, i + 1) for i in range(1, size - 1, 2)]
    far_pairs = far_pairs + [(j, i) for i, j in far_pairs]
    second = lax.ppermute(second, "space", far_pairs)
    first = lax.ppermute(first, "space", [(i, i ^ 1) for i in range(size)])

    listed, params = pl.pallas_call(
        functools.partial(list_kernel, layers=layers, rows=rows, depth=depth),
        out_shape=[
            jax.ShapeDtypeStruct((count + 1,), jnp.int32),
            jax.ShapeDtypeStruct((TILE + 16, 128), f32),
        ],
        in_specs=[SMEM, VMEM, VMEM],
        out_specs=[SMEM, VMEM],
        scratch_shapes=[pltpu.VMEM((TILE, 128), f32)],
        compiler_params=PARAMS,
        name="owned",
    )(receivers, shifts.reshape(1, poles), residues.T)

    def field(slots):
        return pltpu.VMEM((slots, 3, half + TILE, depth), f32)

    basis, sel = pl.pallas_call(
        basis_kernel,
        out_shape=[
            jax.ShapeDtypeStruct((layers * SLOTS * half, depth), f32),
            jax.ShapeDtypeStruct((groups, SLOTS + TILE, 128), f32),
        ],
        in_specs=[VMEM] * 5 + [hbm],
        out_specs=[VMEM, VMEM],
        scratch_shapes=[
            pltpu.VMEM((layers + 4, half + TILE, depth), f32),
            pltpu.VMEM((2, half + TILE, depth), f32),
            pltpu.VMEM((2, half + TILE, depth), f32),
            *[field(layers + 4) for _ in range(6)],
            pltpu.SMEM((count + 1,), jnp.int32),
            pltpu.SemaphoreType.DMA(()),
        ],
        compiler_params=PARAMS,
        name="basis",
    )(own_cond, own_field, own_ends, first, second, listed)
    basis = basis.reshape(layers, SLOTS, half, depth)

    is_end = lax.broadcasted_iota(jnp.int32, sel.shape, 1) >= SLOTS
    stride = 2
    while stride < size:
        other = lax.ppermute(sel, "space", [(i, i ^ stride) for i in range(size)])
        sel = jnp.where(is_end, jnp.maximum(sel, other), sel + other)
        stride *= 2
    ends = sel
    sel = sel[:, :SLOTS]
    other = lax.ppermute(sel, "space", [(i, i ^ 1) for i in range(size)])

    early = layers - 1
    gated_shape = jax.ShapeDtypeStruct((gates, 3, layers, half, depth), f32)
    gated, w = pl.pallas_call(
        functools.partial(gate_kernel, poles=poles),
        grid=(early,),
        out_shape=[gated_shape, jax.ShapeDtypeStruct((WORDS, 16, 128), f32)],
        in_specs=[
            pl.BlockSpec(ends.shape, lambda i: (0, 0, 0)),
            pl.BlockSpec(params.shape, lambda i: (0, 0)),
            pl.BlockSpec((1, SLOTS, half, depth), lambda i: (i, 0, 0, 0)),
        ],
        out_specs=[
            pl.BlockSpec((gates, 3, 1, half, depth), lambda i: (0, 0, i, 0, 0)),
            pl.BlockSpec((WORDS, 16, 128), lambda i: (0, 0, 0)),
        ],
        compiler_params=PARAMS,
        cost_estimate=pl.CostEstimate(flops=2**24, bytes_accessed=2**23, transcendentals=0),
        name="gates",
    )(ends, params, basis)

    sel, w = lax.optimization_barrier((sel + other, w))
    other = lax.ppermute(sel, "pole", [(0, 1), (1, 0)])
    gated = pl.pallas_call(
        rest_kernel,
        grid=(layers - early,),
        out_shape=gated_shape,
        in_specs=[
            pl.BlockSpec(w.shape, lambda i: (0, 0, 0)),
            pl.BlockSpec((1, SLOTS, half, depth), lambda i: (i + early, 0, 0, 0)),
            hbm,
        ],
        out_specs=pl.BlockSpec((gates, 3, 1, half, depth), lambda i: (0, 0, i + early, 0, 0)),
        input_output_aliases={2: 0},
        compiler_params=PARAMS,
        cost_estimate=pl.CostEstimate(flops=2**22, bytes_accessed=2**21, transcendentals=0),
        name="rest",
    )(w, basis, gated)
    sel = sel + other

    traces = pl.pallas_call(
        trace_kernel,
        out_shape=jax.ShapeDtypeStruct((gates, 3, count), f32),
        in_specs=[VMEM, VMEM],
        out_specs=VMEM,
        compiler_params=PARAMS,
        name="traces",
    )(w, sel)
    return gated, traces


def solution(mesh):
    placed = (
        P(("survey", "space"), None, None),
        P(None, ("survey", "space"), None, None),
        P(),
        P(),
        P("survey"),
    )
    return jax.shard_map(
        per_device,
        mesh=mesh,
        in_specs=placed,
        out_specs=(P(None, None, ("survey", "space"), "pole", None), P(None, None, "survey")),
        check_vma=False,
    )
```

```python
import functools

import jax
import jax.numpy as jnp
from jax import lax
from jax.experimental import pallas as pl
from jax.experimental.pallas import tpu as pltpu
from jax.sharding import PartitionSpec as P

MID = 4.65
WORDS = 10
POINTWISE = (0, 2, 5, 9)
FIELDS = (1, 3, 4, 6, 7, 8)
SIGMA = 3 * (1 + len(FIELDS))
ENDS = SIGMA + 1
SLOTS = ENDS + 2
PICKS = 4
TILE = 8
VMEM = pl.BlockSpec(memory_space=pltpu.VMEM)
SMEM = pl.BlockSpec(memory_space=pltpu.SMEM)
PARAMS = pltpu.CompilerParams(vmem_limit_bytes=48 * 1024 * 1024)


def sub_next(v):
    return pltpu.roll(v, v.shape[0] - 1, 0)


def sub_prev(v):
    return pltpu.roll(v, 1, 0)


def lanes_of(v):
    return lax.broadcasted_iota(jnp.int32, v.shape, 1)


def rows_of(v):
    return lax.broadcasted_iota(jnp.int32, v.shape, 0)


def lane_next(v):
    return jnp.where(lanes_of(v) == v.shape[1] - 1, 0.0, pltpu.roll(v, v.shape[1] - 1, 1))


def lane_prev(v, first):
    return jnp.where(lanes_of(v) == 0, first, pltpu.roll(v, 1, 1))


def split(value, size):
    if size & (size - 1):
        return lax.div(value, size), lax.rem(value, size)
    return value >> (size.bit_length() - 1), value & (size - 1)


def bits_of(size):
    return (size - 1).bit_length()


def part_keep(core):
    row = lax.broadcasted_iota(jnp.int32, (TILE, 128), 0)
    return jnp.where(core == 0, (row < 5).astype(jnp.float32), (row >= 5).astype(jnp.float32))


def own_rows(half, core):
    return pl.ds(pl.multiple_of(core * half, TILE), half)


def extra_rows(half, core):
    return pl.ds(pl.multiple_of(half - core * TILE, TILE), TILE)


def to_front(tile, core):
    return jnp.where(core == 0, tile, pltpu.roll(tile, 3, 0))


def from_front(tile, core):
    tile = jnp.where(rows_of(tile) < 3, tile, 0.0)
    return jnp.where(core == 0, tile, pltpu.roll(tile, TILE - 3, 0))


def pack_extras(near, far, ends):
    row = rows_of(ends)
    spare = [
        pltpu.roll(far[0], 6, 0),
        pltpu.roll(far[1], 6, 0),
        jnp.where(row == 6, pltpu.roll(far[0], 4, 0), pltpu.roll(far[1], 5, 0)),
        pltpu.roll(ends, 6, 0),
    ]
    return [
        jnp.where(
            row < 3,
            near[2 * at],
            jnp.where(row < 6, pltpu.roll(near[2 * at + 1], 3, 0), spare[at]),
        )
        for at in range(4)
    ]


def unpack_near(tiles, at, core):
    tile = tiles[at // 2]
    return from_front(pltpu.roll(tile, TILE - 3, 0) if at % 2 else tile, core)


def unpack_far(tiles, at, core):
    last = pltpu.roll(tiles[2], 4 - at, 0)
    return from_front(jnp.where(rows_of(last) < 2, pltpu.roll(tiles[at], 2, 0), last), core)


def send_kernel(cond_hbm, src_hbm, first_ref, second_ref, cond_out, field_out, ends_ref, cond_ref, src_ref, sems):
    core = lax.axis_index("pole")
    odd = lax.rem(lax.axis_index("space"), 2)
    layers, rows, _ = cond_ref.shape
    half = rows // 2
    own, extra = own_rows(half, core), extra_rows(half, core)
    keep = part_keep(core)
    copies = [pltpu.make_async_copy(cond_hbm, cond_ref, sems.at[0])] + [
        pltpu.make_async_copy(src_hbm.at[c], src_ref.at[c], sems.at[1 + c]) for c in range(3)
    ]
    for copy in copies:
        copy.start()
    for copy in copies:
        copy.wait()

    conds, fields = [], []
    for layer in range(layers):
        cond = jnp.concatenate([cond_ref[layer, own, :], cond_ref[layer, extra, :] * keep], axis=0)
        field = [
            cond * jnp.concatenate([src_ref[c, layer, own, :], src_ref[c, layer, extra, :]], axis=0)
            for c in range(3)
        ]
        cond_out[layer] = cond
        for c in range(3):
            field_out[layer, c] = field[c]
        conds.append(cond)
        fields.append(field)

    top = jnp.max(jnp.max(cond_ref[...], axis=0), axis=0, keepdims=True)
    low = jnp.max(-jnp.min(cond_ref[...], axis=0), axis=0, keepdims=True)
    row = lax.broadcasted_iota(jnp.int32, (TILE, 128), 0)
    ends = jnp.where(row == 0, top, low)
    ends_ref[...] = ends
    for upward in (True, False):
        near = [layers - 1, layers - 2] if upward else [0, 1]
        fx, fy, fz = fields[layers - 3 if upward else 2]
        far = [fy + sub_next(fx) - fx, fz + lane_next(fx) - fx] if upward else [fy, fz]
        blocks = [v for layer in near for v in (*fields[layer], conds[layer])] + far
        edges = [to_front(block[half:], core) for block in blocks]
        pairs = pack_extras(edges[:8], edges[8:], ends)

        def write(out_ref):
            for at, block in enumerate(blocks):
                out_ref[at * half : (at + 1) * half, :] = block[:half]
            base = len(blocks) * half
            for at, pair in enumerate(pairs):
                out_ref[base + at * TILE : base + (at + 1) * TILE, :] = pair

        with_first = odd == 0 if upward else odd == 1

        @pl.when(with_first)
        def _():
            write(first_ref)

        @pl.when(jnp.logical_not(with_first))
        def _():
            write(second_ref)


def list_kernel(rec_ref, shifts_ref, res_ref, list_ref, par_ref, square, *, layers, rows, depth):
    core = lax.axis_index("pole")
    base = lax.axis_index("space") * layers
    half = rows // 2
    total = rec_ref.shape[0]

    bits = bits_of(total)

    def step(at, count):
        line, z = split(rec_ref[at], depth)
        x, y = split(line, rows)
        x, y = x - base, y - core * half
        owned = (x >= 0) & (x < layers) & (y >= 0) & (y < half)
        start = x * (SLOTS * half) + y
        turn = (at - z) & 127
        list_ref[count] = (((start << 7) | turn) << bits) | at
        return count + owned.astype(jnp.int32)

    list_ref[total] = lax.fori_loop(0, total, step, jnp.int32(0), unroll=8)
    poles, gates = res_ref.shape
    square[...] = jnp.zeros_like(square)
    square[:poles, :gates] = res_ref[...]
    par_ref[...] = jnp.zeros_like(par_ref)
    par_ref[TILE : TILE + gates, :poles] = square[...].T[:gates, :poles]
    par_ref[:1, :poles] = shifts_ref[...]


def curl_curl(get_u, get, layers, put, half, trimmed=False):
    first = layers[0]
    u_y, u_z = get_u(first - 1)
    _, g, e = get(first, (1, 2))
    prev_z, prev_y = g - u_y, u_z - e
    for layer in layers:
        f, g, e = get(layer, (0, 1, 2))
        _, g_up, e_up = get(layer + 1, (1, 2))
        h_z = g_up - (g + (sub_next(f) - f))
        h_y = (e + (lane_next(f) - f)) - e_up
        h_x = (sub_next(e) - e) - (lane_next(g) - g)
        out_x = (h_z - sub_prev(h_z)) + (lane_prev(h_y, f) - h_y) - 8.0 * f
        out_y = (h_x - lane_prev(h_x, -g)) + (prev_z - h_z) - 8.0 * g
        out_z = (h_y - prev_y) + (sub_prev(h_x) - h_x) - 8.0 * e
        prev_z, prev_y = h_z, h_y
        put(layer, (out_x, out_y, out_z))


def basis_kernel(
    cond_ref, field_ref, ends_ref, first_ref, second_ref, list_hbm,
    bas_ref, sel_ref,
    sig, low3, high3, t00, t10, t11, t20, t21, t22, list_ref, list_sem,
):
    core = lax.axis_index("pole")
    place = lax.axis_index("space")
    odd = lax.rem(place, 2)
    layers, reach, depth = cond_ref.shape
    half = reach - TILE
    keep = part_keep(core)
    list_copy = pltpu.make_async_copy(list_hbm, list_ref, list_sem)
    list_copy.start()
    low_ok = (place > 0).astype(jnp.float32)
    high_ok = (place < lax.axis_size("space") - 1).astype(jnp.float32)

    def received(upward, at):
        part = pl.ds(at * half, half)
        from_first = odd == 1 if upward else odd == 0
        return jnp.where(from_first, first_ref[part, :], second_ref[part, :])

    def received_tile(upward, at):
        part = pl.ds(10 * half + at * TILE, TILE)
        from_first = odd == 1 if upward else odd == 0
        return jnp.where(from_first, first_ref[part, :], second_ref[part, :])

    for layer in range(layers):
        moved = cond_ref[layer] - MID
        sig[layer + 2] = moved
        for c in range(3):
            field = field_ref[layer, c]
            t00[layer + 2, c] = field
            t11[layer + 2, c] = moved * field
    for upward in (True, False):
        tiles = [received_tile(upward, at) for at in range(4)]
        for distance in (1, 2):
            slot = 2 - distance if upward else layers + 1 + distance
            base = (distance - 1) * 4
            moved = jnp.concatenate(
                [received(upward, base + 3), unpack_near(tiles, base + 3, core)], axis=0
            ) - MID
            sig[slot] = moved
            for c in range(3):
                field = jnp.concatenate(
                    [received(upward, base + c), unpack_near(tiles, base + c, core)], axis=0
                )
                t00[slot, c] = field
                t11[slot, c] = moved * field
        far = low3 if upward else high3
        for at in range(2):
            far[at] = jnp.concatenate(
                [received(upward, 8 + at), unpack_far(tiles, at, core)], axis=0
            )

    def sums(ref):
        def get_u(slot):
            f, g, e = ref[slot, 0], ref[slot, 1], ref[slot, 2]
            return g + (sub_next(f) - f), e + (lane_next(f) - f)

        return get_u

    def reader(ref):
        def get(slot, which):
            return [ref[slot, c] if c in which else None for c in range(3)]

        return get

    def inside(slot, value):
        value = jnp.concatenate([value[:half], value[half:] * keep], axis=0)
        if slot < 2:
            return value * low_ok
        if slot > layers + 1:
            return value * high_ok
        return value

    def get_b(slot, which):
        if slot > layers + 3:
            return None, high3[0], high3[1]
        return [t00[slot, c] if c in which else None for c in range(3)]

    def put_10(slot, out):
        for c in range(3):
            t10[slot, c] = inside(slot, out[c])

    curl_curl(lambda slot: (low3[0], low3[1]), get_b, list(range(layers + 4)), put_10, half)

    def put_20(slot, out):
        for c in range(3):
            t20[slot, c] = inside(slot, out[c])

    def put_21(slot, out):
        for c in range(3):
            t21[slot, c] = inside(slot, out[c]) + sig[slot] * t10[slot, c]
            t22[slot, c] = sig[slot] * t11[slot, c]

    middle = list(range(1, layers + 3))
    curl_curl(sums(t10), reader(t10), middle, put_20, half)
    curl_curl(sums(t11), reader(t11), middle, put_21, half)

    def store(word, slot, c, value):
        base = ((slot - 2) * SLOTS + word * 3 + c) * half
        bas_ref[base : base + half, :] = value

    inner = list(range(2, layers + 2))
    for slot in inner:
        for c in range(3):
            for word, ref in enumerate((t00, t10, t20, t21)):
                store(word, slot, c, ref[slot, c, :half, :])
        base = ((slot - 2) * SLOTS + SIGMA) * half
        bas_ref[base : base + half, :] = sig[slot, :half, :]

    def put_3(word, before):
        def put(slot, out):
            for c in range(3):
                value = out[c][:half]
                if before is not None:
                    value = value + sig[slot, :half, :] * before[slot, c, :half, :]
                store(word, slot, c, value)

        return put

    curl_curl(sums(t20), reader(t20), inner, put_3(4, None), half)
    curl_curl(sums(t21), reader(t21), inner, put_3(5, t20), half)
    curl_curl(sums(t22), reader(t22), inner, put_3(6, t21), half)

    groups = sel_ref.shape[0]
    lane = lax.broadcasted_iota(jnp.int32, (SLOTS, depth), 1)
    total = list_ref.shape[0] - 1
    bits = bits_of(total)
    list_copy.wait()
    owned = list_ref[total]

    def pick(turn, found):
        for step in range(PICKS):
            at = turn * PICKS + step
            code = jnp.where(at < owned, list_ref[jnp.minimum(at, total - 1)], 0)
            which = jnp.where(at < owned, code & ((1 << bits) - 1), -1)
            block = bas_ref[pl.ds(code >> (7 + bits), SLOTS, stride=half), :]
            block = pltpu.roll(block, (code >> bits) & 127, 1)
            found = [
                jnp.where(lane == which - 128 * group, block, value)
                for group, value in enumerate(found)
            ]
        return found

    zero = jnp.zeros((SLOTS, depth), jnp.float32)
    found = lax.fori_loop(0, (owned + PICKS - 1) // PICKS, pick, [zero] * groups)
    for group in range(groups):
        sel_ref[group] = found[group]

    tile = first_ref[10 * half + 3 * TILE : 10 * half + 4 * TILE, :]
    for group in range(groups):
        sel_ref[group, ENDS:, :] = jnp.maximum(ends_ref[:2, :], tile[TILE - 2 :])


def weights(ends_ref, par_ref, out_ref, gates, poles):
    upper = jnp.max(ends_ref[0, ENDS : ENDS + 1, :], axis=1, keepdims=True)
    lower = -jnp.max(ends_ref[0, ENDS + 1 : ENDS + 2, :], axis=1, keepdims=True)
    shift = jnp.where(lax.broadcasted_iota(jnp.int32, (1, 128), 1) < poles, par_ref[:1, :], 1.0)
    low_end = shift * lower
    high_end = 16.0 + shift * upper
    center = (high_end + low_end) / 2.0
    spread = (high_end - low_end) / 2.0
    scaled = center / spread
    residual = [jnp.ones_like(shift)]
    direction = [1.0 / center]
    ratio = 1.0 / scaled
    total = list(direction)
    for _ in range(3):
        applied = [center * d for d in direction] + [jnp.zeros_like(shift)]
        for at, d in enumerate(direction):
            applied[at + 1] = applied[at + 1] + spread * d
        residual = [
            (residual[at] if at < len(residual) else 0.0) - a for at, a in enumerate(applied)
        ]
        ratio_new = 1.0 / (2.0 * scaled - ratio)
        grown = [(2.0 * ratio_new / spread) * r for r in residual]
        direction = [
            g + ratio_new * ratio * direction[at] if at < len(direction) else g
            for at, g in enumerate(grown)
        ]
        ratio = ratio_new
        total = [
            d + total[at] if at < len(total) else d for at, d in enumerate(direction)
        ]
    offset = shift * (MID - (upper + lower) / 2.0)
    inverse = 1.0 / spread
    y0, y1, y2, y3 = total
    y1 = y1 * inverse
    y2 = y2 * inverse * inverse
    y3 = y3 * inverse * inverse * inverse
    powers = [
        y0 + offset * (y1 + offset * (y2 + offset * y3)),
        y1 + offset * (2.0 * y2 + 3.0 * offset * y3),
        y2 + 3.0 * offset * y3,
        y3,
    ]
    word = 0
    res = par_ref[TILE : TILE + gates, :]
    for m in range(4):
        term = powers[m]
        for _ in range(m + 1):
            column = jnp.sum(res * term, axis=1, keepdims=True)
            out_ref[word, : res.shape[0], :] = jnp.broadcast_to(column, (res.shape[0], 128))
            term = term * shift
            word += 1


def power_sum(weight, moved):
    total = weight(POINTWISE[3])
    for word in POINTWISE[2::-1]:
        total = total * moved + weight(word)
    return total


def combine(w_ref, bas_ref, out_ref, gates, layer):
    half = bas_ref.shape[2]
    for top in range(0, half, TILE):
        part = slice(top, top + TILE)
        moved = bas_ref[layer, SIGMA, part, :]
        fields = [bas_ref[layer, at, part, :] for at in range(SIGMA)]
        for g in range(gates):
            weight = lambda word: w_ref[word, g : g + 1, :]
            scale = power_sum(weight, moved)
            for c in range(3):
                total = scale * fields[c]
                for at, word in enumerate(FIELDS, 1):
                    total = total + weight(word) * fields[at * 3 + c]
                out_ref[g, c, 0, part, :] = total


def gate_kernel(ends_ref, par_ref, bas_ref, out_ref, w_ref, *, poles):
    gates = out_ref.shape[0]

    @pl.when(pl.program_id(0) == 0)
    def _():
        weights(ends_ref, par_ref, w_ref, gates, poles)

    combine(w_ref, bas_ref, out_ref, gates, pl.program_id(0))


def rest_kernel(w_ref, bas_ref, before_ref, out_ref, *, early):
    del before_ref
    combine(w_ref, bas_ref, out_ref, out_ref.shape[0], pl.program_id(0) + early)


def trace_kernel(w_ref, sel_ref, out_ref):
    gates = out_ref.shape[0]
    weight = lambda word: w_ref[word, :gates, :]
    for group in range(sel_ref.shape[0]):
        scale = power_sum(weight, sel_ref[group, SIGMA : SIGMA + 1, :])
        for c in range(3):
            total = scale * sel_ref[group, c : c + 1, :]
            for at, word in enumerate(FIELDS, 1):
                total = total + weight(word) * sel_ref[group, at * 3 + c : at * 3 + c + 1, :]
            for g in range(gates):
                out_ref[g, c : c + 1, group * 128 : (group + 1) * 128] = total[g : g + 1]


def per_device(conductivity, source_field, shifts, residues, receivers):
    layers, rows, depth = conductivity.shape
    half = rows // 2
    gates, poles = residues.shape
    count = receivers.shape[0]
    groups = count // 128
    size = lax.axis_size("space")
    f32 = jnp.float32
    message = jax.ShapeDtypeStruct((10 * half + 4 * TILE, depth), f32)
    hbm = pl.BlockSpec(memory_space=pltpu.HBM)

    first, second, own_cond, own_field, own_ends = pl.pallas_call(
        send_kernel,
        out_shape=[
            message,
            message,
            jax.ShapeDtypeStruct((layers, half + TILE, depth), f32),
            jax.ShapeDtypeStruct((layers, 3, half + TILE, depth), f32),
            jax.ShapeDtypeStruct((TILE, 128), f32),
        ],
        in_specs=[hbm, hbm],
        out_specs=[VMEM] * 5,
        scratch_shapes=[
            pltpu.VMEM((layers, rows, depth), f32),
            pltpu.VMEM((3, layers, rows, depth), f32),
            pltpu.SemaphoreType.DMA((4,)),
        ],
        compiler_params=pltpu.CompilerParams(vmem_limit_bytes=53 * 1024 * 1024),
        name="send",
    )(conductivity, source_field)
    far_pairs = [(i, i + 1) for i in range(1, size - 1, 2)]
    far_pairs = far_pairs + [(j, i) for i, j in far_pairs]
    second = lax.ppermute(second, "space", far_pairs)
    first = lax.ppermute(first, "space", [(i, i ^ 1) for i in range(size)])

    listed, params = pl.pallas_call(
        functools.partial(list_kernel, layers=layers, rows=rows, depth=depth),
        out_shape=[
            jax.ShapeDtypeStruct((count + 1,), jnp.int32),
            jax.ShapeDtypeStruct((TILE + 16, 128), f32),
        ],
        in_specs=[SMEM, VMEM, VMEM],
        out_specs=[SMEM, VMEM],
        scratch_shapes=[pltpu.VMEM((TILE, 128), f32)],
        compiler_params=PARAMS,
        name="owned",
    )(receivers, shifts.reshape(1, poles), residues.T)

    def field(slots):
        return pltpu.VMEM((slots, 3, half + TILE, depth), f32)

    basis, sel = pl.pallas_call(
        basis_kernel,
        out_shape=[
            jax.ShapeDtypeStruct((layers * SLOTS * half, depth), f32),
            jax.ShapeDtypeStruct((groups, SLOTS, 128), f32),
        ],
        in_specs=[VMEM] * 5 + [hbm],
        out_specs=[VMEM, VMEM],
        scratch_shapes=[
            pltpu.VMEM((layers + 4, half + TILE, depth), f32),
            pltpu.VMEM((2, half + TILE, depth), f32),
            pltpu.VMEM((2, half + TILE, depth), f32),
            *[field(layers + 4) for _ in range(6)],
            pltpu.SMEM((count + 1,), jnp.int32),
            pltpu.SemaphoreType.DMA(()),
        ],
        compiler_params=PARAMS,
        name="basis",
    )(own_cond, own_field, own_ends, first, second, listed)
    basis = basis.reshape(layers, SLOTS, half, depth)

    is_end = lax.broadcasted_iota(jnp.int32, sel.shape, 1) >= ENDS
    stride = 2
    while stride < size:
        other = lax.ppermute(sel, "space", [(i, i ^ stride) for i in range(size)])
        sel = jnp.where(is_end, jnp.maximum(sel, other), sel + other)
        stride *= 2
    ends = sel
    other = lax.ppermute(sel, "space", [(i, i ^ 1) for i in range(size)])

    early = layers - 1
    gated_shape = jax.ShapeDtypeStruct((gates, 3, layers, half, depth), f32)
    gated, w = pl.pallas_call(
        functools.partial(gate_kernel, poles=poles),
        grid=(early,),
        out_shape=[gated_shape, jax.ShapeDtypeStruct((WORDS, 16, 128), f32)],
        in_specs=[
            VMEM,
            VMEM,
            VMEM,
        ],
        out_specs=[
            pl.BlockSpec((gates, 3, 1, half, depth), lambda i: (0, 0, i, 0, 0)),
            pl.BlockSpec((WORDS, 16, 128), lambda i: (0, 0, 0)),
        ],
        compiler_params=PARAMS,
        cost_estimate=pl.CostEstimate(flops=2**24, bytes_accessed=2**23, transcendentals=0),
        name="gates",
    )(ends, params, basis)

    sel, w = lax.optimization_barrier((sel + other, w))
    other = lax.ppermute(sel, "pole", [(0, 1), (1, 0)])
    gated = pl.pallas_call(
        functools.partial(rest_kernel, early=early),
        grid=(layers - early,),
        out_shape=gated_shape,
        in_specs=[
            VMEM,
            VMEM,
            hbm,
        ],
        out_specs=pl.BlockSpec((gates, 3, 1, half, depth), lambda i: (0, 0, i + early, 0, 0)),
        input_output_aliases={2: 0},
        compiler_params=PARAMS,
        cost_estimate=pl.CostEstimate(flops=2**22, bytes_accessed=2**21, transcendentals=0),
        name="rest",
    )(w, basis, gated)
    sel = sel + other

    traces = pl.pallas_call(
        trace_kernel,
        out_shape=jax.ShapeDtypeStruct((gates, 3, count), f32),
        in_specs=[VMEM, VMEM],
        out_specs=VMEM,
        compiler_params=PARAMS,
        name="traces",
    )(w, sel)
    return gated, traces


def solution(mesh):
    placed = (
        P(("survey", "space"), None, None),
        P(None, ("survey", "space"), None, None),
        P(),
        P(),
        P("survey"),
    )
    return jax.shard_map(
        per_device,
        mesh=mesh,
        in_specs=placed,
        out_specs=(P(None, None, ("survey", "space"), "pole", None), P(None, None, "survey")),
        check_vma=False,
    )
```

```python
import functools

import jax
import jax.numpy as jnp
from jax import lax
from jax.experimental import pallas as pl
from jax.experimental.pallas import tpu as pltpu
from jax.sharding import PartitionSpec as P

MID = 4.65
WORDS = 10
POINTWISE = (0, 2, 5, 9)
FIELDS = (1, 3, 4, 6, 7, 8)
SIGMA = 3 * (1 + len(FIELDS))
ENDS = SIGMA + 1
SLOTS = ENDS + 2
PICKS = 4
TILE = 8
VMEM = pl.BlockSpec(memory_space=pltpu.VMEM)
SMEM = pl.BlockSpec(memory_space=pltpu.SMEM)
PARAMS = pltpu.CompilerParams(vmem_limit_bytes=48 * 1024 * 1024)


def sub_next(v):
    return pltpu.roll(v, v.shape[0] - 1, 0)


def sub_prev(v):
    return pltpu.roll(v, 1, 0)


def lanes_of(v):
    return lax.broadcasted_iota(jnp.int32, v.shape, 1)


def rows_of(v):
    return lax.broadcasted_iota(jnp.int32, v.shape, 0)


def lane_next(v):
    return jnp.where(lanes_of(v) == v.shape[1] - 1, 0.0, pltpu.roll(v, v.shape[1] - 1, 1))


def lane_prev(v, first):
    return jnp.where(lanes_of(v) == 0, first, pltpu.roll(v, 1, 1))


def split(value, size):
    if size & (size - 1):
        return lax.div(value, size), lax.rem(value, size)
    return value >> (size.bit_length() - 1), value & (size - 1)


def bits_of(size):
    return (size - 1).bit_length()


def part_keep(core):
    row = lax.broadcasted_iota(jnp.int32, (TILE, 128), 0)
    return jnp.where(core == 0, (row < 5).astype(jnp.float32), (row >= 5).astype(jnp.float32))


def own_rows(half, core):
    return pl.ds(pl.multiple_of(core * half, TILE), half)


def extra_rows(half, core):
    return pl.ds(pl.multiple_of(half - core * TILE, TILE), TILE)


def to_front(tile, core):
    return jnp.where(core == 0, tile, pltpu.roll(tile, 3, 0))


def from_front(tile, core):
    tile = jnp.where(rows_of(tile) < 3, tile, 0.0)
    return jnp.where(core == 0, tile, pltpu.roll(tile, TILE - 3, 0))


def pack_extras(near, far, ends):
    row = rows_of(ends)
    spare = [
        pltpu.roll(far[0], 6, 0),
        pltpu.roll(far[1], 6, 0),
        jnp.where(row == 6, pltpu.roll(far[0], 4, 0), pltpu.roll(far[1], 5, 0)),
        pltpu.roll(ends, 6, 0),
    ]
    return [
        jnp.where(
            row < 3,
            near[2 * at],
            jnp.where(row < 6, pltpu.roll(near[2 * at + 1], 3, 0), spare[at]),
        )
        for at in range(4)
    ]


def unpack_near(tiles, at, core):
    tile = tiles[at // 2]
    return from_front(pltpu.roll(tile, TILE - 3, 0) if at % 2 else tile, core)


def unpack_far(tiles, at, core):
    last = pltpu.roll(tiles[2], 4 - at, 0)
    return from_front(jnp.where(rows_of(last) < 2, pltpu.roll(tiles[at], 2, 0), last), core)


def send_kernel(all_ref, first_ref, second_ref, cond_out, field_out, ends_ref):
    core = lax.axis_index("pole")
    odd = lax.rem(lax.axis_index("space"), 2)
    _, layers, rows, _ = all_ref.shape
    half = rows // 2
    own, extra = own_rows(half, core), extra_rows(half, core)
    keep = part_keep(core)
    conds, fields = [], []
    for layer in range(layers):
        *field, cond = [
            jnp.concatenate([all_ref[c, layer, own, :], all_ref[c, layer, extra, :] * keep], axis=0)
            for c in range(4)
        ]
        cond_out[layer] = cond
        for c in range(3):
            field_out[layer, c] = field[c]
        conds.append(cond)
        fields.append(field)

    top = jnp.max(jnp.max(all_ref[3], axis=0), axis=0, keepdims=True)
    low = jnp.max(-jnp.min(all_ref[3], axis=0), axis=0, keepdims=True)
    row = lax.broadcasted_iota(jnp.int32, (TILE, 128), 0)
    ends = jnp.where(row == 0, top, low)
    ends_ref[...] = ends
    for upward in (True, False):
        near = [layers - 1, layers - 2] if upward else [0, 1]
        fx, fy, fz = fields[layers - 3 if upward else 2]
        far = [fy + sub_next(fx) - fx, fz + lane_next(fx) - fx] if upward else [fy, fz]
        blocks = [v for layer in near for v in (*fields[layer], conds[layer])] + far
        edges = [to_front(block[half:], core) for block in blocks]
        pairs = pack_extras(edges[:8], edges[8:], ends)

        def write(out_ref):
            for at, block in enumerate(blocks):
                out_ref[at * half : (at + 1) * half, :] = block[:half]
            base = len(blocks) * half
            for at, pair in enumerate(pairs):
                out_ref[base + at * TILE : base + (at + 1) * TILE, :] = pair

        with_first = odd == 0 if upward else odd == 1

        @pl.when(with_first)
        def _():
            write(first_ref)

        @pl.when(jnp.logical_not(with_first))
        def _():
            write(second_ref)


def list_kernel(rec_ref, shifts_ref, res_ref, list_ref, par_ref, square, *, layers, rows, depth):
    core = lax.axis_index("pole")
    base = lax.axis_index("space") * layers
    half = rows // 2
    total = rec_ref.shape[0]

    bits = bits_of(total)

    def step(at, count):
        line, z = split(rec_ref[at], depth)
        x, y = split(line, rows)
        x, y = x - base, y - core * half
        owned = (x >= 0) & (x < layers) & (y >= 0) & (y < half)
        start = x * (SLOTS * half) + y
        turn = (at - z) & 127
        list_ref[count] = (((start << 7) | turn) << bits) | at
        return count + owned.astype(jnp.int32)

    list_ref[total] = lax.fori_loop(0, total, step, jnp.int32(0), unroll=8)
    poles, gates = res_ref.shape
    square[...] = jnp.zeros_like(square)
    square[:poles, :gates] = res_ref[...]
    par_ref[...] = jnp.zeros_like(par_ref)
    par_ref[TILE : TILE + gates, :poles] = square[...].T[:gates, :poles]
    par_ref[:1, :poles] = shifts_ref[...]


def curl_curl(get_u, get, layers, put, half, trimmed=False):
    first = layers[0]
    u_y, u_z = get_u(first - 1)
    _, g, e = get(first, (1, 2))
    prev_z, prev_y = g - u_y, u_z - e
    for layer in layers:
        f, g, e = get(layer, (0, 1, 2))
        _, g_up, e_up = get(layer + 1, (1, 2))
        h_z = g_up - (g + (sub_next(f) - f))
        h_y = (e + (lane_next(f) - f)) - e_up
        h_x = (sub_next(e) - e) - (lane_next(g) - g)
        out_x = (h_z - sub_prev(h_z)) + (lane_prev(h_y, f) - h_y) - 8.0 * f
        out_y = (h_x - lane_prev(h_x, -g)) + (prev_z - h_z) - 8.0 * g
        out_z = (h_y - prev_y) + (sub_prev(h_x) - h_x) - 8.0 * e
        prev_z, prev_y = h_z, h_y
        put(layer, (out_x, out_y, out_z))


def basis_kernel(
    cond_ref, field_ref, ends_ref, first_ref, second_ref, list_hbm,
    bas_ref, sel_ref,
    sig, low3, high3, t00, t10, t11, t20, t21, t22, list_ref, list_sem,
):
    core = lax.axis_index("pole")
    place = lax.axis_index("space")
    odd = lax.rem(place, 2)
    layers, reach, depth = cond_ref.shape
    half = reach - TILE
    keep = part_keep(core)
    list_copy = pltpu.make_async_copy(list_hbm, list_ref, list_sem)
    list_copy.start()
    low_ok = (place > 0).astype(jnp.float32)
    high_ok = (place < lax.axis_size("space") - 1).astype(jnp.float32)

    def received(upward, at):
        part = pl.ds(at * half, half)
        from_first = odd == 1 if upward else odd == 0
        return jnp.where(from_first, first_ref[part, :], second_ref[part, :])

    def received_tile(upward, at):
        part = pl.ds(10 * half + at * TILE, TILE)
        from_first = odd == 1 if upward else odd == 0
        return jnp.where(from_first, first_ref[part, :], second_ref[part, :])

    for layer in range(layers):
        moved = cond_ref[layer] - MID
        sig[layer + 2] = moved
        for c in range(3):
            field = field_ref[layer, c]
            t00[layer + 2, c] = field
            t11[layer + 2, c] = moved * field
    for upward in (True, False):
        tiles = [received_tile(upward, at) for at in range(4)]
        for distance in (1, 2):
            slot = 2 - distance if upward else layers + 1 + distance
            base = (distance - 1) * 4
            moved = jnp.concatenate(
                [received(upward, base + 3), unpack_near(tiles, base + 3, core)], axis=0
            ) - MID
            sig[slot] = moved
            for c in range(3):
                field = jnp.concatenate(
                    [received(upward, base + c), unpack_near(tiles, base + c, core)], axis=0
                )
                t00[slot, c] = field
                t11[slot, c] = moved * field
        far = low3 if upward else high3
        for at in range(2):
            far[at] = jnp.concatenate(
                [received(upward, 8 + at), unpack_far(tiles, at, core)], axis=0
            )

    def sums(ref):
        def get_u(slot):
            f, g, e = ref[slot, 0], ref[slot, 1], ref[slot, 2]
            return g + (sub_next(f) - f), e + (lane_next(f) - f)

        return get_u

    def reader(ref):
        def get(slot, which):
            return [ref[slot, c] if c in which else None for c in range(3)]

        return get

    def inside(slot, value):
        value = jnp.concatenate([value[:half], value[half:] * keep], axis=0)
        if slot < 2:
            return value * low_ok
        if slot > layers + 1:
            return value * high_ok
        return value

    def get_b(slot, which):
        if slot > layers + 3:
            return None, high3[0], high3[1]
        return [t00[slot, c] if c in which else None for c in range(3)]

    def put_10(slot, out):
        for c in range(3):
            t10[slot, c] = inside(slot, out[c])

    curl_curl(lambda slot: (low3[0], low3[1]), get_b, list(range(layers + 4)), put_10, half)

    def put_20(slot, out):
        for c in range(3):
            t20[slot, c] = inside(slot, out[c])

    def put_21(slot, out):
        for c in range(3):
            t21[slot, c] = inside(slot, out[c]) + sig[slot] * t10[slot, c]
            t22[slot, c] = sig[slot] * t11[slot, c]

    middle = list(range(1, layers + 3))
    curl_curl(sums(t10), reader(t10), middle, put_20, half)
    curl_curl(sums(t11), reader(t11), middle, put_21, half)

    def store(word, slot, c, value):
        base = ((slot - 2) * SLOTS + word * 3 + c) * half
        bas_ref[base : base + half, :] = value

    inner = list(range(2, layers + 2))
    for slot in inner:
        for c in range(3):
            for word, ref in enumerate((t00, t10, t20, t21)):
                store(word, slot, c, ref[slot, c, :half, :])
        base = ((slot - 2) * SLOTS + SIGMA) * half
        bas_ref[base : base + half, :] = sig[slot, :half, :]

    def put_3(word, before):
        def put(slot, out):
            for c in range(3):
                value = out[c][:half]
                if before is not None:
                    value = value + sig[slot, :half, :] * before[slot, c, :half, :]
                store(word, slot, c, value)

        return put

    curl_curl(sums(t20), reader(t20), inner, put_3(4, None), half)
    curl_curl(sums(t21), reader(t21), inner, put_3(5, t20), half)
    curl_curl(sums(t22), reader(t22), inner, put_3(6, t21), half)

    groups = sel_ref.shape[0]
    lane = lax.broadcasted_iota(jnp.int32, (SLOTS, depth), 1)
    total = list_ref.shape[0] - 1
    bits = bits_of(total)
    list_copy.wait()
    owned = list_ref[total]

    def pick(turn, found):
        for step in range(PICKS):
            at = turn * PICKS + step
            code = jnp.where(at < owned, list_ref[jnp.minimum(at, total - 1)], 0)
            which = jnp.where(at < owned, code & ((1 << bits) - 1), -1)
            block = bas_ref[pl.ds(code >> (7 + bits), SLOTS, stride=half), :]
            block = pltpu.roll(block, (code >> bits) & 127, 1)
            found = [
                jnp.where(lane == which - 128 * group, block, value)
                for group, value in enumerate(found)
            ]
        return found

    zero = jnp.zeros((SLOTS, depth), jnp.float32)
    found = lax.fori_loop(0, (owned + PICKS - 1) // PICKS, pick, [zero] * groups)
    for group in range(groups):
        sel_ref[group] = found[group]

    tile = first_ref[10 * half + 3 * TILE : 10 * half + 4 * TILE, :]
    for group in range(groups):
        sel_ref[group, ENDS:, :] = jnp.maximum(ends_ref[:2, :], tile[TILE - 2 :])


def weights(ends_ref, par_ref, out_ref, gates, poles):
    upper = jnp.max(ends_ref[0, ENDS : ENDS + 1, :], axis=1, keepdims=True)
    lower = -jnp.max(ends_ref[0, ENDS + 1 : ENDS + 2, :], axis=1, keepdims=True)
    shift = jnp.where(lax.broadcasted_iota(jnp.int32, (1, 128), 1) < poles, par_ref[:1, :], 1.0)
    low_end = shift * lower
    high_end = 16.0 + shift * upper
    center = (high_end + low_end) / 2.0
    spread = (high_end - low_end) / 2.0
    scaled = center / spread
    residual = [jnp.ones_like(shift)]
    direction = [1.0 / center]
    ratio = 1.0 / scaled
    total = list(direction)
    for _ in range(3):
        applied = [center * d for d in direction] + [jnp.zeros_like(shift)]
        for at, d in enumerate(direction):
            applied[at + 1] = applied[at + 1] + spread * d
        residual = [
            (residual[at] if at < len(residual) else 0.0) - a for at, a in enumerate(applied)
        ]
        ratio_new = 1.0 / (2.0 * scaled - ratio)
        grown = [(2.0 * ratio_new / spread) * r for r in residual]
        direction = [
            g + ratio_new * ratio * direction[at] if at < len(direction) else g
            for at, g in enumerate(grown)
        ]
        ratio = ratio_new
        total = [
            d + total[at] if at < len(total) else d for at, d in enumerate(direction)
        ]
    offset = shift * (MID - (upper + lower) / 2.0)
    inverse = 1.0 / spread
    y0, y1, y2, y3 = total
    y1 = y1 * inverse
    y2 = y2 * inverse * inverse
    y3 = y3 * inverse * inverse * inverse
    powers = [
        y0 + offset * (y1 + offset * (y2 + offset * y3)),
        y1 + offset * (2.0 * y2 + 3.0 * offset * y3),
        y2 + 3.0 * offset * y3,
        y3,
    ]
    word = 0
    res = par_ref[TILE : TILE + gates, :]
    for m in range(4):
        term = powers[m]
        for _ in range(m + 1):
            column = jnp.sum(res * term, axis=1, keepdims=True)
            out_ref[word, : res.shape[0], :] = jnp.broadcast_to(column, (res.shape[0], 128))
            term = term * shift
            word += 1


def power_sum(weight, moved):
    total = weight(POINTWISE[3])
    for word in POINTWISE[2::-1]:
        total = total * moved + weight(word)
    return total


def combine(w_ref, bas_ref, out_ref, gates, layer):
    half = bas_ref.shape[2]
    for top in range(0, half, TILE):
        part = slice(top, top + TILE)
        moved = bas_ref[layer, SIGMA, part, :]
        fields = [bas_ref[layer, at, part, :] for at in range(SIGMA)]
        for g in range(gates):
            weight = lambda word: w_ref[word, g : g + 1, :]
            scale = power_sum(weight, moved)
            for c in range(3):
                total = scale * fields[c]
                for at, word in enumerate(FIELDS, 1):
                    total = total + weight(word) * fields[at * 3 + c]
                out_ref[g, c, 0, part, :] = total


def gate_kernel(ends_ref, par_ref, bas_ref, out_ref, w_ref, *, poles):
    gates = out_ref.shape[0]

    @pl.when(pl.program_id(0) == 0)
    def _():
        weights(ends_ref, par_ref, w_ref, gates, poles)

    combine(w_ref, bas_ref, out_ref, gates, pl.program_id(0))


def rest_kernel(w_ref, bas_ref, before_ref, out_ref, *, early):
    del before_ref
    combine(w_ref, bas_ref, out_ref, out_ref.shape[0], pl.program_id(0) + early)


def trace_kernel(w_ref, sel_ref, out_ref):
    gates = out_ref.shape[0]
    weight = lambda word: w_ref[word, :gates, :]
    for group in range(sel_ref.shape[0]):
        scale = power_sum(weight, sel_ref[group, SIGMA : SIGMA + 1, :])
        for c in range(3):
            total = scale * sel_ref[group, c : c + 1, :]
            for at, word in enumerate(FIELDS, 1):
                total = total + weight(word) * sel_ref[group, at * 3 + c : at * 3 + c + 1, :]
            for g in range(gates):
                out_ref[g, c : c + 1, group * 128 : (group + 1) * 128] = total[g : g + 1]


def per_device(conductivity, source_field, shifts, residues, receivers):
    layers, rows, depth = conductivity.shape
    half = rows // 2
    gates, poles = residues.shape
    count = receivers.shape[0]
    groups = count // 128
    size = lax.axis_size("space")
    f32 = jnp.float32
    message = jax.ShapeDtypeStruct((10 * half + 4 * TILE, depth), f32)
    hbm = pl.BlockSpec(memory_space=pltpu.HBM)

    first, second, own_cond, own_field, own_ends = pl.pallas_call(
        send_kernel,
        out_shape=[
            message,
            message,
            jax.ShapeDtypeStruct((layers, half + TILE, depth), f32),
            jax.ShapeDtypeStruct((layers, 3, half + TILE, depth), f32),
            jax.ShapeDtypeStruct((TILE, 128), f32),
        ],
        in_specs=[VMEM],
        out_specs=[VMEM] * 5,
        compiler_params=pltpu.CompilerParams(vmem_limit_bytes=48 * 1024 * 1024),
        name="send",
    )(conductivity * jnp.pad(source_field, ((0, 1), (0, 0), (0, 0), (0, 0)), constant_values=1.0))
    far_pairs = [(i, i + 1) for i in range(1, size - 1, 2)]
    far_pairs = far_pairs + [(j, i) for i, j in far_pairs]
    second = lax.ppermute(second, "space", far_pairs)
    first = lax.ppermute(first, "space", [(i, i ^ 1) for i in range(size)])

    listed, params = pl.pallas_call(
        functools.partial(list_kernel, layers=layers, rows=rows, depth=depth),
        out_shape=[
            jax.ShapeDtypeStruct((count + 1,), jnp.int32),
            jax.ShapeDtypeStruct((TILE + 16, 128), f32),
        ],
        in_specs=[SMEM, VMEM, VMEM],
        out_specs=[SMEM, VMEM],
        scratch_shapes=[pltpu.VMEM((TILE, 128), f32)],
        compiler_params=PARAMS,
        name="owned",
    )(receivers, shifts.reshape(1, poles), residues.T)

    def field(slots):
        return pltpu.VMEM((slots, 3, half + TILE, depth), f32)

    basis, sel = pl.pallas_call(
        basis_kernel,
        out_shape=[
            jax.ShapeDtypeStruct((layers * SLOTS * half, depth), f32),
            jax.ShapeDtypeStruct((groups, SLOTS, 128), f32),
        ],
        in_specs=[VMEM] * 5 + [hbm],
        out_specs=[VMEM, VMEM],
        scratch_shapes=[
            pltpu.VMEM((layers + 4, half + TILE, depth), f32),
            pltpu.VMEM((2, half + TILE, depth), f32),
            pltpu.VMEM((2, half + TILE, depth), f32),
            *[field(layers + 4) for _ in range(6)],
            pltpu.SMEM((count + 1,), jnp.int32),
            pltpu.SemaphoreType.DMA(()),
        ],
        compiler_params=PARAMS,
        name="basis",
    )(own_cond, own_field, own_ends, first, second, listed)
    basis = basis.reshape(layers, SLOTS, half, depth)

    is_end = lax.broadcasted_iota(jnp.int32, sel.shape, 1) >= ENDS
    stride = 2
    while stride < size:
        other = lax.ppermute(sel, "space", [(i, i ^ stride) for i in range(size)])
        sel = jnp.where(is_end, jnp.maximum(sel, other), sel + other)
        stride *= 2
    ends = sel
    other = lax.ppermute(sel, "space", [(i, i ^ 1) for i in range(size)])

    early = layers - 1
    gated_shape = jax.ShapeDtypeStruct((gates, 3, layers, half, depth), f32)
    gated, w = pl.pallas_call(
        functools.partial(gate_kernel, poles=poles),
        grid=(early,),
        out_shape=[gated_shape, jax.ShapeDtypeStruct((WORDS, 16, 128), f32)],
        in_specs=[
            VMEM,
            VMEM,
            VMEM,
        ],
        out_specs=[
            pl.BlockSpec((gates, 3, 1, half, depth), lambda i: (0, 0, i, 0, 0)),
            pl.BlockSpec((WORDS, 16, 128), lambda i: (0, 0, 0)),
        ],
        compiler_params=PARAMS,
        cost_estimate=pl.CostEstimate(flops=2**24, bytes_accessed=2**23, transcendentals=0),
        name="gates",
    )(ends, params, basis)

    sel, w = lax.optimization_barrier((sel + other, w))
    other = lax.ppermute(sel, "pole", [(0, 1), (1, 0)])
    gated = pl.pallas_call(
        functools.partial(rest_kernel, early=early),
        grid=(layers - early,),
        out_shape=gated_shape,
        in_specs=[
            VMEM,
            VMEM,
            hbm,
        ],
        out_specs=pl.BlockSpec((gates, 3, 1, half, depth), lambda i: (0, 0, i + early, 0, 0)),
        input_output_aliases={2: 0},
        compiler_params=PARAMS,
        cost_estimate=pl.CostEstimate(flops=2**22, bytes_accessed=2**21, transcendentals=0),
        name="rest",
    )(w, basis, gated)
    sel = sel + other

    traces = pl.pallas_call(
        trace_kernel,
        out_shape=jax.ShapeDtypeStruct((gates, 3, count), f32),
        in_specs=[VMEM, VMEM],
        out_specs=VMEM,
        compiler_params=PARAMS,
        name="traces",
    )(w, sel)
    return gated, traces


def solution(mesh):
    placed = (
        P(("survey", "space"), None, None),
        P(None, ("survey", "space"), None, None),
        P(),
        P(),
        P("survey"),
    )
    return jax.shard_map(
        per_device,
        mesh=mesh,
        in_specs=placed,
        out_specs=(P(None, None, ("survey", "space"), "pole", None), P(None, None, "survey")),
        check_vma=False,
    )
```

```python
import functools

import jax
import jax.numpy as jnp
from jax import lax
from jax.experimental import pallas as pl
from jax.experimental.pallas import tpu as pltpu
from jax.sharding import PartitionSpec as P

MID = 4.65
WORDS = 10
POINTWISE = (0, 2, 5, 9)
FIELDS = (1, 3, 4, 6, 7, 8)
SIGMA = 3 * (1 + len(FIELDS))
ENDS = SIGMA + 1
SLOTS = ENDS + 2
PICKS = 4
TILE = 8
VMEM = pl.BlockSpec(memory_space=pltpu.VMEM)
SMEM = pl.BlockSpec(memory_space=pltpu.SMEM)
PARAMS = pltpu.CompilerParams(vmem_limit_bytes=48 * 1024 * 1024)


def sub_next(v):
    return pltpu.roll(v, v.shape[0] - 1, 0)


def sub_prev(v):
    return pltpu.roll(v, 1, 0)


def lanes_of(v):
    return lax.broadcasted_iota(jnp.int32, v.shape, 1)


def rows_of(v):
    return lax.broadcasted_iota(jnp.int32, v.shape, 0)


def lane_next(v):
    return jnp.where(lanes_of(v) == v.shape[1] - 1, 0.0, pltpu.roll(v, v.shape[1] - 1, 1))


def lane_prev(v, first):
    return jnp.where(lanes_of(v) == 0, first, pltpu.roll(v, 1, 1))


def split(value, size):
    if size & (size - 1):
        return lax.div(value, size), lax.rem(value, size)
    return value >> (size.bit_length() - 1), value & (size - 1)


def bits_of(size):
    return (size - 1).bit_length()


def part_keep(core):
    row = lax.broadcasted_iota(jnp.int32, (TILE, 128), 0)
    return jnp.where(core == 0, (row < 5).astype(jnp.float32), (row >= 5).astype(jnp.float32))


def own_rows(half, core):
    return pl.ds(pl.multiple_of(core * half, TILE), half)


def extra_rows(half, core):
    return pl.ds(pl.multiple_of(half - core * TILE, TILE), TILE)


def to_front(tile, core):
    return jnp.where(core == 0, tile, pltpu.roll(tile, 3, 0))


def from_front(tile, core):
    tile = jnp.where(rows_of(tile) < 3, tile, 0.0)
    return jnp.where(core == 0, tile, pltpu.roll(tile, TILE - 3, 0))


def pack_extras(near, far, ends):
    row = rows_of(ends)
    spare = [
        pltpu.roll(far[0], 6, 0),
        pltpu.roll(far[1], 6, 0),
        jnp.where(row == 6, pltpu.roll(far[0], 4, 0), pltpu.roll(far[1], 5, 0)),
        pltpu.roll(ends, 6, 0),
    ]
    return [
        jnp.where(
            row < 3,
            near[2 * at],
            jnp.where(row < 6, pltpu.roll(near[2 * at + 1], 3, 0), spare[at]),
        )
        for at in range(4)
    ]


def unpack_near(tiles, at, core):
    tile = tiles[at // 2]
    return from_front(pltpu.roll(tile, TILE - 3, 0) if at % 2 else tile, core)


def unpack_far(tiles, at, core):
    last = pltpu.roll(tiles[2], 4 - at, 0)
    return from_front(jnp.where(rows_of(last) < 2, pltpu.roll(tiles[at], 2, 0), last), core)


def send_kernel(all_ref, first_ref, second_ref, cond_out, field_out, ends_ref):
    core = lax.axis_index("pole")
    odd = lax.rem(lax.axis_index("space"), 2)
    _, layers, rows, _ = all_ref.shape
    half = rows // 2
    own, extra = own_rows(half, core), extra_rows(half, core)
    keep = part_keep(core)
    conds, fields = [], []
    for layer in range(layers):
        *field, cond = [
            jnp.concatenate([all_ref[c, layer, own, :], all_ref[c, layer, extra, :] * keep], axis=0)
            for c in range(4)
        ]
        cond_out[layer] = cond
        for c in range(3):
            field_out[layer, c] = field[c]
        conds.append(cond)
        fields.append(field)

    top = jnp.max(jnp.max(all_ref[3], axis=0), axis=0, keepdims=True)
    low = jnp.max(-jnp.min(all_ref[3], axis=0), axis=0, keepdims=True)
    row = lax.broadcasted_iota(jnp.int32, (TILE, 128), 0)
    ends = jnp.where(row == 0, top, low)
    ends_ref[...] = ends
    for upward in (True, False):
        near = [layers - 1, layers - 2] if upward else [0, 1]
        fx, fy, fz = fields[layers - 3 if upward else 2]
        far = [fy + sub_next(fx) - fx, fz + lane_next(fx) - fx] if upward else [fy, fz]
        blocks = [v for layer in near for v in (*fields[layer], conds[layer])] + far
        edges = [to_front(block[half:], core) for block in blocks]
        pairs = pack_extras(edges[:8], edges[8:], ends)

        def write(out_ref):
            for at, block in enumerate(blocks):
                out_ref[at * half : (at + 1) * half, :] = block[:half]
            base = len(blocks) * half
            for at, pair in enumerate(pairs):
                out_ref[base + at * TILE : base + (at + 1) * TILE, :] = pair

        with_first = odd == 0 if upward else odd == 1

        @pl.when(with_first)
        def _():
            write(first_ref)

        @pl.when(jnp.logical_not(with_first))
        def _():
            write(second_ref)


def curl_curl(get_u, get, layers, put):
    first = layers[0]
    u_y, u_z = get_u(first - 1)
    _, g, e = get(first, (1, 2))
    prev_z, prev_y = g - u_y, u_z - e
    for layer in layers:
        f, g, e = get(layer, (0, 1, 2))
        _, g_up, e_up = get(layer + 1, (1, 2))
        h_z = g_up - (g + (sub_next(f) - f))
        h_y = (e + (lane_next(f) - f)) - e_up
        h_x = (sub_next(e) - e) - (lane_next(g) - g)
        out_x = (h_z - sub_prev(h_z)) + (lane_prev(h_y, f) - h_y) - 8.0 * f
        out_y = (h_x - lane_prev(h_x, -g)) + (prev_z - h_z) - 8.0 * g
        out_z = (h_y - prev_y) + (sub_prev(h_x) - h_x) - 8.0 * e
        prev_z, prev_y = h_z, h_y
        put(layer, (out_x, out_y, out_z))


def own_kernel(code_ref, cond_ref, field_ref, list_ref, sig_ref, one_ref, mixed_ref, twice_ref, t11, t22):
    layers, reach, depth = cond_ref.shape
    blank = jnp.zeros((reach, depth), jnp.float32)
    for layer in range(layers):
        moved = cond_ref[layer] - MID
        sig_ref[layer] = moved
        for c in range(3):
            once = moved * field_ref[layer, c]
            t11[layer, c] = once
            t22[layer, c] = moved * once

    def apply(src, out):
        def get(layer, which):
            if layer == layers:
                return [blank] * 3
            return [src[layer, c] if c in which else None for c in range(3)]

        def put(layer, values):
            for c in range(3):
                out[layer, c] = values[c]

        curl_curl(lambda layer: (blank, blank), get, list(range(layers)), put)

    apply(field_ref, one_ref)
    apply(t11, mixed_ref)
    apply(t22, twice_ref)

    total = code_ref.shape[0]

    def step(at, count):
        code = code_ref[at]
        list_ref[count] = code
        return count + (code >= 0).astype(jnp.int32)

    list_ref[total] = lax.fori_loop(0, total, step, jnp.int32(0), unroll=8)


def basis_kernel(
    field_ref, sig_ref, one_ref, mixed_ref, twice_ref, ends_ref, first_ref, second_ref, list_hbm,
    bas_ref, sel_ref,
    sig, low3, high3, t00, t11, t10, t20, t21, list_ref, list_sem,
):
    core = lax.axis_index("pole")
    place = lax.axis_index("space")
    odd = lax.rem(place, 2)
    layers, _, reach, depth = field_ref.shape
    half = reach - TILE
    keep = part_keep(core)
    list_copy = pltpu.make_async_copy(list_hbm, list_ref, list_sem)
    list_copy.start()
    low_ok = (place > 0).astype(jnp.float32)
    high_ok = (place < lax.axis_size("space") - 1).astype(jnp.float32)
    first, last = 2, layers + 1
    inner = list(range(first, last + 1))

    def received(upward, start, size):
        part = pl.ds(start, size)
        from_first = odd == 1 if upward else odd == 0
        return jnp.where(from_first, first_ref[part, :], second_ref[part, :])

    for upward in (True, False):
        tiles = [received(upward, 10 * half + at * TILE, TILE) for at in range(4)]
        blocks = [received(upward, at * half, half) for at in range(10)]
        near = [
            jnp.concatenate([blocks[at], unpack_near(tiles, at, core)], axis=0) for at in range(8)
        ]
        for distance in (1, 2):
            slot = first - distance if upward else last + distance
            base = (distance - 1) * 4
            moved = near[base + 3] - MID
            sig[slot] = moved
            for c in range(3):
                t00[slot, c] = near[base + c]
                t11[slot, c] = moved * near[base + c]
        far = low3 if upward else high3
        for at in range(2):
            far[at] = jnp.concatenate([blocks[8 + at], unpack_far(tiles, at, core)], axis=0)
    for slot in (first, last):
        for c in range(3):
            t11[slot, c] = sig_ref[slot - first] * field_ref[slot - first, c]

    def get_b(slot, which):
        if slot > last + 2:
            return None, high3[0], high3[1]
        if slot in inner:
            return [field_ref[slot - first, c] if c in which else None for c in range(3)]
        return [t00[slot, c] if c in which else None for c in range(3)]

    def reader(ref):
        def get(slot, which):
            return [ref[slot, c] if c in which else None for c in range(3)]

        return get

    def sums(get):
        def get_u(slot):
            if slot < 0:
                return low3[0], low3[1]
            f, g, e = get(slot, (0, 1, 2))
            return g + (sub_next(f) - f), e + (lane_next(f) - f)

        return get_u

    def inside(slot, value):
        value = jnp.concatenate([value[:half], value[half:] * keep], axis=0)
        if slot < first:
            return value * low_ok
        if slot > last:
            return value * high_ok
        return value

    def completed(part_ref, slot, get):
        out = [part_ref[slot - first, c] for c in range(3)]
        if slot == first:
            u_y, u_z = sums(get)(slot - 1)
            out[1] = out[1] - u_y
            out[2] = out[2] - u_z
        if slot == last:
            _, g, e = get(slot + 1, (1, 2))
            out[0] = out[0] + (g - sub_prev(g)) + (e - lane_prev(e, 0.0))
            out[1] = out[1] - g
            out[2] = out[2] - e
        return out

    def put_10(slot, out):
        for c in range(3):
            t10[slot, c] = inside(slot, out[c])

    def put_21(slot, out):
        moved = sig_ref[slot - first] if slot in inner else sig[slot]
        for c in range(3):
            t21[slot, c] = inside(slot, out[c]) + moved * t10[slot, c]

    def put_20(slot, out):
        for c in range(3):
            t20[slot, c] = inside(slot, out[c])

    curl_curl(sums(get_b), get_b, [0, 1], put_10)
    curl_curl(sums(get_b), get_b, [last + 1, last + 2], put_10)
    for slot in inner:
        put_10(slot, completed(one_ref, slot, get_b))
    get_11 = reader(t11)
    curl_curl(sums(get_11), get_11, [first - 1], put_21)
    curl_curl(sums(get_11), get_11, [last + 1], put_21)
    for slot in inner:
        put_21(slot, completed(mixed_ref, slot, get_11))
    get_10 = reader(t10)
    curl_curl(sums(get_10), get_10, list(range(first - 1, last + 2)), put_20)

    def store(word, slot, c, value):
        base = ((slot - first) * SLOTS + word * 3 + c) * half
        bas_ref[base : base + half, :] = value

    for slot in inner:
        for c in range(3):
            store(0, slot, c, field_ref[slot - first, c, :half, :])
            for word, ref in enumerate((t10, t20, t21), 1):
                store(word, slot, c, ref[slot, c, :half, :])
        base = ((slot - first) * SLOTS + SIGMA) * half
        bas_ref[base : base + half, :] = sig_ref[slot - first, :half, :]

    def put_3(word, before):
        def put(slot, out):
            for c in range(3):
                value = out[c][:half]
                if before is not None:
                    moved = sig_ref[slot - first, :half, :]
                    value = value + moved * before[slot, c, :half, :]
                store(word, slot, c, value)

        return put

    get_20, get_21 = reader(t20), reader(t21)
    curl_curl(sums(get_20), get_20, inner, put_3(4, None))
    curl_curl(sums(get_21), get_21, inner, put_3(5, t20))

    def get_22(slot, which):
        return [sig[slot] * t11[slot, c] if c in which else None for c in range(3)]

    for slot in inner:
        put_3(6, t21)(slot, completed(twice_ref, slot, get_22))

    groups = sel_ref.shape[0]
    lane = lax.broadcasted_iota(jnp.int32, (SLOTS, depth), 1)
    total = list_ref.shape[0] - 1
    bits = bits_of(total)
    list_copy.wait()
    owned = list_ref[total]

    def pick(turn, found):
        for step in range(PICKS):
            at = turn * PICKS + step
            code = jnp.where(at < owned, list_ref[jnp.minimum(at, total - 1)], 0)
            which = jnp.where(at < owned, code & ((1 << bits) - 1), -1)
            block = bas_ref[pl.ds(code >> (7 + bits), SLOTS, stride=half), :]
            block = pltpu.roll(block, (code >> bits) & 127, 1)
            found = [
                jnp.where(lane == which - 128 * group, block, value)
                for group, value in enumerate(found)
            ]
        return found

    zero = jnp.zeros((SLOTS, depth), jnp.float32)
    found = lax.fori_loop(0, (owned + PICKS - 1) // PICKS, pick, [zero] * groups)
    for group in range(groups):
        sel_ref[group] = found[group]

    tile = first_ref[10 * half + 3 * TILE : 10 * half + 4 * TILE, :]
    for group in range(groups):
        sel_ref[group, ENDS:, :] = jnp.maximum(ends_ref[:2, :], tile[TILE - 2 :])


def weights(ends_ref, par_ref, out_ref, gates, poles):
    upper = jnp.max(ends_ref[0, ENDS : ENDS + 1, :], axis=1, keepdims=True)
    lower = -jnp.max(ends_ref[0, ENDS + 1 : ENDS + 2, :], axis=1, keepdims=True)
    shift = jnp.where(lax.broadcasted_iota(jnp.int32, (1, 128), 1) < poles, par_ref[:1, :], 1.0)
    low_end = shift * lower
    high_end = 16.0 + shift * upper
    center = (high_end + low_end) / 2.0
    spread = (high_end - low_end) / 2.0
    scaled = center / spread
    residual = [jnp.ones_like(shift)]
    direction = [1.0 / center]
    ratio = 1.0 / scaled
    total = list(direction)
    for _ in range(3):
        applied = [center * d for d in direction] + [jnp.zeros_like(shift)]
        for at, d in enumerate(direction):
            applied[at + 1] = applied[at + 1] + spread * d
        residual = [
            (residual[at] if at < len(residual) else 0.0) - a for at, a in enumerate(applied)
        ]
        ratio_new = 1.0 / (2.0 * scaled - ratio)
        grown = [(2.0 * ratio_new / spread) * r for r in residual]
        direction = [
            g + ratio_new * ratio * direction[at] if at < len(direction) else g
            for at, g in enumerate(grown)
        ]
        ratio = ratio_new
        total = [
            d + total[at] if at < len(total) else d for at, d in enumerate(direction)
        ]
    offset = shift * (MID - (upper + lower) / 2.0)
    inverse = 1.0 / spread
    y0, y1, y2, y3 = total
    y1 = y1 * inverse
    y2 = y2 * inverse * inverse
    y3 = y3 * inverse * inverse * inverse
    powers = [
        y0 + offset * (y1 + offset * (y2 + offset * y3)),
        y1 + offset * (2.0 * y2 + 3.0 * offset * y3),
        y2 + 3.0 * offset * y3,
        y3,
    ]
    word = 0
    res = par_ref[TILE : TILE + gates, :]
    for m in range(4):
        term = powers[m]
        for _ in range(m + 1):
            column = jnp.sum(res * term, axis=1, keepdims=True)
            out_ref[word, : res.shape[0], :] = jnp.broadcast_to(column, (res.shape[0], 128))
            term = term * shift
            word += 1


def power_sum(weight, moved):
    total = weight(POINTWISE[3])
    for word in POINTWISE[2::-1]:
        total = total * moved + weight(word)
    return total


def combine(w_ref, bas_ref, out_ref, gates, layer):
    half = bas_ref.shape[2]
    for top in range(0, half, TILE):
        part = slice(top, top + TILE)
        moved = bas_ref[layer, SIGMA, part, :]
        fields = [bas_ref[layer, at, part, :] for at in range(SIGMA)]
        for g in range(gates):
            weight = lambda word: w_ref[word, g : g + 1, :]
            scale = power_sum(weight, moved)
            for c in range(3):
                total = scale * fields[c]
                for at, word in enumerate(FIELDS, 1):
                    total = total + weight(word) * fields[at * 3 + c]
                out_ref[g, c, 0, part, :] = total


def gate_kernel(ends_ref, par_ref, bas_ref, out_ref, w_ref, *, poles):
    gates = out_ref.shape[0]

    @pl.when(pl.program_id(0) == 0)
    def _():
        weights(ends_ref, par_ref, w_ref, gates, poles)

    combine(w_ref, bas_ref, out_ref, gates, pl.program_id(0))


def rest_kernel(w_ref, bas_ref, before_ref, out_ref, *, early):
    del before_ref
    combine(w_ref, bas_ref, out_ref, out_ref.shape[0], pl.program_id(0) + early)


def trace_kernel(w_ref, sel_ref, out_ref):
    gates = out_ref.shape[0]
    weight = lambda word: w_ref[word, :gates, :]
    for group in range(sel_ref.shape[0]):
        scale = power_sum(weight, sel_ref[group, SIGMA : SIGMA + 1, :])
        for c in range(3):
            total = scale * sel_ref[group, c : c + 1, :]
            for at, word in enumerate(FIELDS, 1):
                total = total + weight(word) * sel_ref[group, at * 3 + c : at * 3 + c + 1, :]
            for g in range(gates):
                out_ref[g, c : c + 1, group * 128 : (group + 1) * 128] = total[g : g + 1]


def per_device(conductivity, source_field, shifts, residues, receivers):
    layers, rows, depth = conductivity.shape
    half = rows // 2
    gates, poles = residues.shape
    count = receivers.shape[0]
    groups = count // 128
    size = lax.axis_size("space")
    f32 = jnp.float32
    message = jax.ShapeDtypeStruct((10 * half + 4 * TILE, depth), f32)
    hbm = pl.BlockSpec(memory_space=pltpu.HBM)

    first, second, own_cond, own_field, own_ends = pl.pallas_call(
        send_kernel,
        out_shape=[
            message,
            message,
            jax.ShapeDtypeStruct((layers, half + TILE, depth), f32),
            jax.ShapeDtypeStruct((layers, 3, half + TILE, depth), f32),
            jax.ShapeDtypeStruct((TILE, 128), f32),
        ],
        in_specs=[VMEM],
        out_specs=[VMEM] * 5,
        compiler_params=pltpu.CompilerParams(vmem_limit_bytes=48 * 1024 * 1024),
        name="send",
    )(conductivity * jnp.pad(source_field, ((0, 1), (0, 0), (0, 0), (0, 0)), constant_values=1.0))
    far_pairs = [(i, i + 1) for i in range(1, size - 1, 2)]
    far_pairs = far_pairs + [(j, i) for i, j in far_pairs]
    second = lax.ppermute(second, "space", far_pairs)
    first = lax.ppermute(first, "space", [(i, i ^ 1) for i in range(size)])

    line, z = receivers // depth, receivers % depth
    x = line // rows - lax.axis_index("space") * layers
    y = line % rows - lax.axis_index("pole") * half
    owned = (x >= 0) & (x < layers) & (y >= 0) & (y < half)
    order = lax.iota(jnp.int32, count)
    codes = (((x * (SLOTS * half) + y) << 7) | ((order - z) & 127)) << bits_of(count) | order
    codes = jnp.where(owned, codes, -1)
    params = jnp.pad(
        jnp.concatenate([jnp.pad(shifts[None], ((0, TILE - 1), (0, 0))), residues]),
        ((0, 16 - gates), (0, 128 - poles)),
    )

    own_shape = jax.ShapeDtypeStruct((layers, 3, half + TILE, depth), f32)
    listed, own_sig, own_one, own_mixed, own_twice = pl.pallas_call(
        own_kernel,
        out_shape=[
            jax.ShapeDtypeStruct((count + 1,), jnp.int32),
            jax.ShapeDtypeStruct((layers, half + TILE, depth), f32),
            own_shape,
            own_shape,
            own_shape,
        ],
        in_specs=[SMEM, VMEM, VMEM],
        out_specs=[SMEM] + [VMEM] * 4,
        scratch_shapes=[pltpu.VMEM(own_shape.shape, f32)] * 2,
        compiler_params=PARAMS,
        cost_estimate=pl.CostEstimate(flops=2**23, bytes_accessed=2**22, transcendentals=0),
        name="owned",
    )(codes, own_cond, own_field)

    def field(slots):
        return pltpu.VMEM((slots, 3, half + TILE, depth), f32)

    basis, sel = pl.pallas_call(
        basis_kernel,
        out_shape=[
            jax.ShapeDtypeStruct((layers * SLOTS * half, depth), f32),
            jax.ShapeDtypeStruct((groups, SLOTS, 128), f32),
        ],
        in_specs=[VMEM] * 8 + [hbm],
        out_specs=[VMEM, VMEM],
        scratch_shapes=[
            pltpu.VMEM((layers + 4, half + TILE, depth), f32),
            pltpu.VMEM((2, half + TILE, depth), f32),
            pltpu.VMEM((2, half + TILE, depth), f32),
            *[field(layers + 4) for _ in range(5)],
            pltpu.SMEM((count + 1,), jnp.int32),
            pltpu.SemaphoreType.DMA(()),
        ],
        compiler_params=PARAMS,
        name="basis",
    )(own_field, own_sig, own_one, own_mixed, own_twice, own_ends, first, second, listed)
    basis = basis.reshape(layers, SLOTS, half, depth)

    is_end = lax.broadcasted_iota(jnp.int32, sel.shape, 1) >= ENDS
    stride = 2
    while stride < size:
        other = lax.ppermute(sel, "space", [(i, i ^ stride) for i in range(size)])
        sel = jnp.where(is_end, jnp.maximum(sel, other), sel + other)
        stride *= 2
    ends = sel
    other = lax.ppermute(sel, "space", [(i, i ^ 1) for i in range(size)])

    early = layers - 1
    gated_shape = jax.ShapeDtypeStruct((gates, 3, layers, half, depth), f32)
    gated, w = pl.pallas_call(
        functools.partial(gate_kernel, poles=poles),
        grid=(early,),
        out_shape=[gated_shape, jax.ShapeDtypeStruct((WORDS, 16, 128), f32)],
        in_specs=[
            VMEM,
            VMEM,
            VMEM,
        ],
        out_specs=[
            pl.BlockSpec((gates, 3, 1, half, depth), lambda i: (0, 0, i, 0, 0)),
            pl.BlockSpec((WORDS, 16, 128), lambda i: (0, 0, 0)),
        ],
        compiler_params=PARAMS,
        cost_estimate=pl.CostEstimate(flops=2**24, bytes_accessed=2**23, transcendentals=0),
        name="gates",
    )(ends, params, basis)

    sel, w = lax.optimization_barrier((sel + other, w))
    other = lax.ppermute(sel, "pole", [(0, 1), (1, 0)])
    gated = pl.pallas_call(
        functools.partial(rest_kernel, early=early),
        grid=(layers - early,),
        out_shape=gated_shape,
        in_specs=[
            VMEM,
            VMEM,
            hbm,
        ],
        out_specs=pl.BlockSpec((gates, 3, 1, half, depth), lambda i: (0, 0, i + early, 0, 0)),
        input_output_aliases={2: 0},
        compiler_params=PARAMS,
        cost_estimate=pl.CostEstimate(flops=2**22, bytes_accessed=2**21, transcendentals=0),
        name="rest",
    )(w, basis, gated)
    sel = sel + other

    traces = pl.pallas_call(
        trace_kernel,
        out_shape=jax.ShapeDtypeStruct((gates, 3, count), f32),
        in_specs=[VMEM, VMEM],
        out_specs=VMEM,
        compiler_params=PARAMS,
        name="traces",
    )(w, sel)
    return gated, traces


def solution(mesh):
    placed = (
        P(("survey", "space"), None, None),
        P(None, ("survey", "space"), None, None),
        P(),
        P(),
        P("survey"),
    )
    return jax.shard_map(
        per_device,
        mesh=mesh,
        in_specs=placed,
        out_specs=(P(None, None, ("survey", "space"), "pole", None), P(None, None, "survey")),
        check_vma=False,
    )
```

```python
import functools

import jax
import jax.numpy as jnp
from jax import lax
from jax.experimental import pallas as pl
from jax.experimental.pallas import tpu as pltpu
from jax.sharding import PartitionSpec as P

MID = 4.65
WORDS = 10
POINTWISE = (0, 2, 5, 9)
FIELDS = (1, 3, 4, 6, 7, 8)
SIGMA = 3 * (1 + len(FIELDS))
ENDS = SIGMA + 1
SLOTS = ENDS + 2
GROUP = 4
LATE = 24
PICKS = 8
TILE = 8
VMEM = pl.BlockSpec(memory_space=pltpu.VMEM)
SMEM = pl.BlockSpec(memory_space=pltpu.SMEM)
PARAMS = pltpu.CompilerParams(vmem_limit_bytes=48 * 1024 * 1024)


def sub_next(v):
    return pltpu.roll(v, v.shape[0] - 1, 0)


def sub_prev(v):
    return pltpu.roll(v, 1, 0)


def lanes_of(v):
    return lax.broadcasted_iota(jnp.int32, v.shape, 1)


def rows_of(v):
    return lax.broadcasted_iota(jnp.int32, v.shape, 0)


def lane_next(v):
    return jnp.where(lanes_of(v) == v.shape[1] - 1, 0.0, pltpu.roll(v, v.shape[1] - 1, 1))


def lane_prev(v, first):
    return jnp.where(lanes_of(v) == 0, first, pltpu.roll(v, 1, 1))


def split(value, size):
    if size & (size - 1):
        return lax.div(value, size), lax.rem(value, size)
    return value >> (size.bit_length() - 1), value & (size - 1)


def bits_of(size):
    return (size - 1).bit_length()


def part_keep(core):
    row = lax.broadcasted_iota(jnp.int32, (TILE, 128), 0)
    return jnp.where(core == 0, (row < 5).astype(jnp.float32), (row >= 5).astype(jnp.float32))


def own_rows(half, core):
    return pl.ds(pl.multiple_of(core * half, TILE), half)


def extra_rows(half, core):
    return pl.ds(pl.multiple_of(half - core * TILE, TILE), TILE)


def to_front(tile, core):
    return jnp.where(core == 0, tile, pltpu.roll(tile, 3, 0))


def from_front(tile, core):
    tile = jnp.where(rows_of(tile) < 3, tile, 0.0)
    return jnp.where(core == 0, tile, pltpu.roll(tile, TILE - 3, 0))


def pack_extras(near, far, ends):
    row = rows_of(ends)
    spare = [
        pltpu.roll(far[0], 6, 0),
        pltpu.roll(far[1], 6, 0),
        jnp.where(row == 6, pltpu.roll(far[0], 4, 0), pltpu.roll(far[1], 5, 0)),
        pltpu.roll(ends, 6, 0),
    ]
    return [
        jnp.where(
            row < 3,
            near[2 * at],
            jnp.where(row < 6, pltpu.roll(near[2 * at + 1], 3, 0), spare[at]),
        )
        for at in range(4)
    ]


def unpack_near(tiles, at, core):
    tile = tiles[at // 2]
    return from_front(pltpu.roll(tile, TILE - 3, 0) if at % 2 else tile, core)


def unpack_far(tiles, at, core):
    last = pltpu.roll(tiles[2], 4 - at, 0)
    return from_front(jnp.where(rows_of(last) < 2, pltpu.roll(tiles[at], 2, 0), last), core)


def send_kernel(all_ref, first_ref, second_ref, cond_out, field_out, ends_ref):
    core = lax.axis_index("pole")
    odd = lax.rem(lax.axis_index("space"), 2)
    _, layers, rows, _ = all_ref.shape
    half = rows // 2
    own, extra = own_rows(half, core), extra_rows(half, core)
    keep = part_keep(core)
    conds, fields = [], []
    for layer in range(layers):
        *field, cond = [
            jnp.concatenate([all_ref[c, layer, own, :], all_ref[c, layer, extra, :] * keep], axis=0)
            for c in range(4)
        ]
        cond_out[layer] = cond
        for c in range(3):
            field_out[layer, c] = field[c]
        conds.append(cond)
        fields.append(field)

    top = jnp.max(jnp.max(all_ref[3], axis=0), axis=0, keepdims=True)
    low = jnp.max(-jnp.min(all_ref[3], axis=0), axis=0, keepdims=True)
    row = lax.broadcasted_iota(jnp.int32, (TILE, 128), 0)
    ends = jnp.where(row == 0, top, low)
    ends_ref[...] = ends
    for upward in (True, False):
        near = [layers - 1, layers - 2] if upward else [0, 1]
        fx, fy, fz = fields[layers - 3 if upward else 2]
        far = [fy + sub_next(fx) - fx, fz + lane_next(fx) - fx] if upward else [fy, fz]
        blocks = [v for layer in near for v in (*fields[layer], conds[layer])] + far
        edges = [to_front(block[half:], core) for block in blocks]
        pairs = pack_extras(edges[:8], edges[8:], ends)

        def write(out_ref):
            for at, block in enumerate(blocks):
                out_ref[at * half : (at + 1) * half, :] = block[:half]
            base = len(blocks) * half
            for at, pair in enumerate(pairs):
                out_ref[base + at * TILE : base + (at + 1) * TILE, :] = pair

        with_first = odd == 0 if upward else odd == 1

        @pl.when(with_first)
        def _():
            write(first_ref)

        @pl.when(jnp.logical_not(with_first))
        def _():
            write(second_ref)


def curl_curl(get_u, get, layers, put):
    first = layers[0]
    u_y, u_z = get_u(first - 1)
    _, g, e = get(first, (1, 2))
    prev_z, prev_y = g - u_y, u_z - e
    for layer in layers:
        f, g, e = get(layer, (0, 1, 2))
        _, g_up, e_up = get(layer + 1, (1, 2))
        h_z = g_up - (g + (sub_next(f) - f))
        h_y = (e + (lane_next(f) - f)) - e_up
        h_x = (sub_next(e) - e) - (lane_next(g) - g)
        out_x = (h_z - sub_prev(h_z)) + (lane_prev(h_y, f) - h_y) - 8.0 * f
        out_y = (h_x - lane_prev(h_x, -g)) + (prev_z - h_z) - 8.0 * g
        out_z = (h_y - prev_y) + (sub_prev(h_x) - h_x) - 8.0 * e
        prev_z, prev_y = h_z, h_y
        put(layer, (out_x, out_y, out_z))


def own_kernel(code_ref, cond_ref, field_ref, list_ref, sig_ref, one_ref, mixed_ref, twice_ref, t11, t22):
    layers, reach, depth = cond_ref.shape
    blank = jnp.zeros((reach, depth), jnp.float32)
    for layer in range(layers):
        moved = cond_ref[layer] - MID
        sig_ref[layer] = moved
        for c in range(3):
            once = moved * field_ref[layer, c]
            t11[layer, c] = once
            t22[layer, c] = moved * once

    def apply(src, out):
        def get(layer, which):
            if layer == layers:
                return [blank] * 3
            return [src[layer, c] if c in which else None for c in range(3)]

        def put(layer, values):
            for c in range(3):
                out[layer, c] = values[c]

        curl_curl(lambda layer: (blank, blank), get, list(range(layers)), put)

    apply(field_ref, one_ref)
    apply(t11, mixed_ref)
    apply(t22, twice_ref)

    total = code_ref.shape[0]

    def step(at, count):
        code = code_ref[at]
        list_ref[count] = code
        return count + (code >= 0).astype(jnp.int32)

    list_ref[total] = lax.fori_loop(0, total, step, jnp.int32(0), unroll=8)


def basis_kernel(
    field_ref, sig_ref, one_ref, mixed_ref, twice_ref, ends_ref, first_ref, second_ref, list_hbm,
    bas_ref, sel_ref,
    sig, low3, high3, t00, t11, t10, t20, t21, list_ref, list_sem,
):
    core = lax.axis_index("pole")
    place = lax.axis_index("space")
    odd = lax.rem(place, 2)
    layers, _, reach, depth = field_ref.shape
    half = reach - TILE
    keep = part_keep(core)
    list_copy = pltpu.make_async_copy(list_hbm, list_ref, list_sem)
    list_copy.start()
    low_ok = (place > 0).astype(jnp.float32)
    high_ok = (place < lax.axis_size("space") - 1).astype(jnp.float32)
    first, last = 2, layers + 1
    inner = list(range(first, last + 1))

    def received(upward, start, size):
        part = pl.ds(start, size)
        from_first = odd == 1 if upward else odd == 0
        return jnp.where(from_first, first_ref[part, :], second_ref[part, :])

    for upward in (True, False):
        tiles = [received(upward, 10 * half + at * TILE, TILE) for at in range(4)]
        blocks = [received(upward, at * half, half) for at in range(10)]
        near = [
            jnp.concatenate([blocks[at], unpack_near(tiles, at, core)], axis=0) for at in range(8)
        ]
        for distance in (1, 2):
            slot = first - distance if upward else last + distance
            base = (distance - 1) * 4
            moved = near[base + 3] - MID
            sig[slot] = moved
            for c in range(3):
                t00[slot, c] = near[base + c]
                t11[slot, c] = moved * near[base + c]
        far = low3 if upward else high3
        for at in range(2):
            far[at] = jnp.concatenate([blocks[8 + at], unpack_far(tiles, at, core)], axis=0)
    for slot in (first, last):
        for c in range(3):
            t11[slot, c] = sig_ref[slot - first] * field_ref[slot - first, c]

    def get_b(slot, which):
        if slot > last + 2:
            return None, high3[0], high3[1]
        if slot in inner:
            return [field_ref[slot - first, c] if c in which else None for c in range(3)]
        return [t00[slot, c] if c in which else None for c in range(3)]

    def reader(ref):
        def get(slot, which):
            return [ref[slot, c] if c in which else None for c in range(3)]

        return get

    def sums(get):
        def get_u(slot):
            if slot < 0:
                return low3[0], low3[1]
            f, g, e = get(slot, (0, 1, 2))
            return g + (sub_next(f) - f), e + (lane_next(f) - f)

        return get_u

    def inside(slot, value):
        value = jnp.concatenate([value[:half], value[half:] * keep], axis=0)
        if slot < first:
            return value * low_ok
        if slot > last:
            return value * high_ok
        return value

    def completed(part_ref, slot, get):
        out = [part_ref[slot - first, c] for c in range(3)]
        if slot == first:
            u_y, u_z = sums(get)(slot - 1)
            out[1] = out[1] - u_y
            out[2] = out[2] - u_z
        if slot == last:
            _, g, e = get(slot + 1, (1, 2))
            out[0] = out[0] + (g - sub_prev(g)) + (e - lane_prev(e, 0.0))
            out[1] = out[1] - g
            out[2] = out[2] - e
        return out

    def put_10(slot, out):
        for c in range(3):
            t10[slot, c] = inside(slot, out[c])

    def put_21(slot, out):
        moved = sig_ref[slot - first] if slot in inner else sig[slot]
        for c in range(3):
            t21[slot, c] = inside(slot, out[c]) + moved * t10[slot, c]

    def put_20(slot, out):
        for c in range(3):
            t20[slot, c] = inside(slot, out[c])

    curl_curl(sums(get_b), get_b, [0, 1], put_10)
    curl_curl(sums(get_b), get_b, [last + 1, last + 2], put_10)
    for slot in inner:
        put_10(slot, completed(one_ref, slot, get_b))
    get_11 = reader(t11)
    curl_curl(sums(get_11), get_11, [first - 1], put_21)
    curl_curl(sums(get_11), get_11, [last + 1], put_21)
    for slot in inner:
        put_21(slot, completed(mixed_ref, slot, get_11))
    get_10 = reader(t10)
    curl_curl(sums(get_10), get_10, list(range(first - 1, last + 2)), put_20)

    def store(word, slot, c, value):
        base = ((slot - first) * SLOTS + word * 3 + c) * half
        bas_ref[base : base + half, :] = value

    for slot in inner:
        for c in range(3):
            store(0, slot, c, field_ref[slot - first, c, :half, :])
            for word, ref in enumerate((t10, t20, t21), 1):
                store(word, slot, c, ref[slot, c, :half, :])
        base = ((slot - first) * SLOTS + SIGMA) * half
        bas_ref[base : base + half, :] = sig_ref[slot - first, :half, :]

    def put_3(word, before):
        def put(slot, out):
            for c in range(3):
                value = out[c][:half]
                if before is not None:
                    moved = sig_ref[slot - first, :half, :]
                    value = value + moved * before[slot, c, :half, :]
                store(word, slot, c, value)

        return put

    get_20, get_21 = reader(t20), reader(t21)
    curl_curl(sums(get_20), get_20, inner, put_3(4, None))
    curl_curl(sums(get_21), get_21, inner, put_3(5, t20))

    def get_22(slot, which):
        return [sig[slot] * t11[slot, c] if c in which else None for c in range(3)]

    for slot in inner:
        put_3(6, t21)(slot, completed(twice_ref, slot, get_22))

    groups = sel_ref.shape[0]
    lane = lax.broadcasted_iota(jnp.int32, (SLOTS, depth), 1)
    total = list_ref.shape[0] - 1
    bits = bits_of(total)
    list_copy.wait()
    owned = list_ref[total]

    def pick(turn, found):
        for step in range(PICKS):
            at = turn * PICKS + step
            code = jnp.where(at < owned, list_ref[jnp.minimum(at, total - 1)], 0)
            which = jnp.where(at < owned, code & ((1 << bits) - 1), -1)
            block = bas_ref[pl.ds(code >> (7 + bits), SLOTS, stride=half), :]
            block = pltpu.roll(block, (code >> bits) & 127, 1)
            found = [
                jnp.where(lane == which - 128 * group, block, value)
                for group, value in enumerate(found)
            ]
        return found

    zero = jnp.zeros((SLOTS, depth), jnp.float32)
    found = lax.fori_loop(0, (owned + PICKS - 1) // PICKS, pick, [zero] * groups)
    for group in range(groups):
        sel_ref[group] = found[group]

    tile = first_ref[10 * half + 3 * TILE : 10 * half + 4 * TILE, :]
    for group in range(groups):
        sel_ref[group, ENDS:, :] = jnp.maximum(ends_ref[:2, :], tile[TILE - 2 :])


def weights(ends_ref, par_ref, out_ref, gates, poles):
    upper = jnp.max(ends_ref[0, ENDS : ENDS + 1, :], axis=1, keepdims=True)
    lower = -jnp.max(ends_ref[0, ENDS + 1 : ENDS + 2, :], axis=1, keepdims=True)
    shift = jnp.where(lax.broadcasted_iota(jnp.int32, (1, 128), 1) < poles, par_ref[:1, :], 1.0)
    low_end = shift * lower
    high_end = 16.0 + shift * upper
    center = (high_end + low_end) / 2.0
    spread = (high_end - low_end) / 2.0
    scaled = center / spread
    residual = [jnp.ones_like(shift)]
    direction = [1.0 / center]
    ratio = 1.0 / scaled
    total = list(direction)
    for _ in range(3):
        applied = [center * d for d in direction] + [jnp.zeros_like(shift)]
        for at, d in enumerate(direction):
            applied[at + 1] = applied[at + 1] + spread * d
        residual = [
            (residual[at] if at < len(residual) else 0.0) - a for at, a in enumerate(applied)
        ]
        ratio_new = 1.0 / (2.0 * scaled - ratio)
        grown = [(2.0 * ratio_new / spread) * r for r in residual]
        direction = [
            g + ratio_new * ratio * direction[at] if at < len(direction) else g
            for at, g in enumerate(grown)
        ]
        ratio = ratio_new
        total = [
            d + total[at] if at < len(total) else d for at, d in enumerate(direction)
        ]
    offset = shift * (MID - (upper + lower) / 2.0)
    inverse = 1.0 / spread
    y0, y1, y2, y3 = total
    y1 = y1 * inverse
    y2 = y2 * inverse * inverse
    y3 = y3 * inverse * inverse * inverse
    powers = [
        y0 + offset * (y1 + offset * (y2 + offset * y3)),
        y1 + offset * (2.0 * y2 + 3.0 * offset * y3),
        y2 + 3.0 * offset * y3,
        y3,
    ]
    word = 0
    res = par_ref[TILE : TILE + gates, :]
    for m in range(4):
        term = powers[m]
        for _ in range(m + 1):
            column = jnp.sum(res * term, axis=1, keepdims=True)
            out_ref[word, : res.shape[0], :] = jnp.broadcast_to(column, (res.shape[0], 128))
            term = term * shift
            word += 1


def power_sum(weight, moved):
    total = weight(POINTWISE[3])
    for word in POINTWISE[2::-1]:
        total = total * moved + weight(word)
    return total


def combine(w_ref, bas_ref, out_hbm, buffer, sems, blocks):
    gates = out_hbm.shape[0]
    copies = []
    for at, (layer, begin, end) in enumerate(blocks):
        for low in range(0, gates, GROUP):
            some = range(low, min(low + GROUP, gates))
            for top in range(begin, end, TILE):
                part = slice(top, top + TILE)
                moved = bas_ref[layer, SIGMA, part, :]
                fields = [bas_ref[layer, row, part, :] for row in range(SIGMA)]
                for g in some:
                    weight = lambda word: w_ref[word, g : g + 1, :]
                    scale = power_sum(weight, moved)
                    for c in range(3):
                        total = scale * fields[c]
                        for row, word in enumerate(FIELDS, 1):
                            total = total + weight(word) * fields[row * 3 + c]
                        buffer[at, g, c, part, :] = total
            rows = pl.ds(begin, end - begin)
            for g in some:
                copy = pltpu.make_async_copy(
                    buffer.at[at, g, :, rows], out_hbm.at[g, :, layer, rows], sems.at[at, g]
                )
                copy.start()
                copies.append(copy)
    for copy in copies:
        copy.wait()


def gate_kernel(ends_ref, par_ref, bas_ref, out_hbm, w_ref, buffer, sems, *, poles, blocks):
    weights(ends_ref, par_ref, w_ref, out_hbm.shape[0], poles)
    combine(w_ref, bas_ref, out_hbm, buffer, sems, blocks)


def rest_kernel(w_ref, bas_ref, before_ref, out_hbm, buffer, sems, *, blocks):
    del before_ref
    combine(w_ref, bas_ref, out_hbm, buffer, sems, blocks)


def trace_kernel(w_ref, sel_ref, out_ref):
    gates = out_ref.shape[0]
    weight = lambda word: w_ref[word, :gates, :]
    for group in range(sel_ref.shape[0]):
        scale = power_sum(weight, sel_ref[group, SIGMA : SIGMA + 1, :])
        for c in range(3):
            total = scale * sel_ref[group, c : c + 1, :]
            for at, word in enumerate(FIELDS, 1):
                total = total + weight(word) * sel_ref[group, at * 3 + c : at * 3 + c + 1, :]
            for g in range(gates):
                out_ref[g, c : c + 1, group * 128 : (group + 1) * 128] = total[g : g + 1]


def per_device(conductivity, source_field, shifts, residues, receivers):
    layers, rows, depth = conductivity.shape
    half = rows // 2
    gates, poles = residues.shape
    count = receivers.shape[0]
    groups = count // 128
    size = lax.axis_size("space")
    f32 = jnp.float32
    message = jax.ShapeDtypeStruct((10 * half + 4 * TILE, depth), f32)
    hbm = pl.BlockSpec(memory_space=pltpu.HBM)

    first, second, own_cond, own_field, own_ends = pl.pallas_call(
        send_kernel,
        out_shape=[
            message,
            message,
            jax.ShapeDtypeStruct((layers, half + TILE, depth), f32),
            jax.ShapeDtypeStruct((layers, 3, half + TILE, depth), f32),
            jax.ShapeDtypeStruct((TILE, 128), f32),
        ],
        in_specs=[VMEM],
        out_specs=[VMEM] * 5,
        compiler_params=pltpu.CompilerParams(vmem_limit_bytes=48 * 1024 * 1024),
        name="send",
    )(conductivity * jnp.pad(source_field, ((0, 1), (0, 0), (0, 0), (0, 0)), constant_values=1.0))
    far_pairs = [(i, i + 1) for i in range(1, size - 1, 2)]
    far_pairs = far_pairs + [(j, i) for i, j in far_pairs]
    second = lax.ppermute(second, "space", far_pairs)
    first = lax.ppermute(first, "space", [(i, i ^ 1) for i in range(size)])

    line, z = receivers // depth, receivers % depth
    x = line // rows - lax.axis_index("space") * layers
    y = line % rows - lax.axis_index("pole") * half
    owned = (x >= 0) & (x < layers) & (y >= 0) & (y < half)
    order = lax.iota(jnp.int32, count)
    codes = (((x * (SLOTS * half) + y) << 7) | ((order - z) & 127)) << bits_of(count) | order
    codes = jnp.where(owned, codes, -1)
    params = jnp.pad(
        jnp.concatenate([jnp.pad(shifts[None], ((0, TILE - 1), (0, 0))), residues]),
        ((0, 16 - gates), (0, 128 - poles)),
    )

    own_shape = jax.ShapeDtypeStruct((layers, 3, half + TILE, depth), f32)
    listed, own_sig, own_one, own_mixed, own_twice = pl.pallas_call(
        own_kernel,
        out_shape=[
            jax.ShapeDtypeStruct((count + 1,), jnp.int32),
            jax.ShapeDtypeStruct((layers, half + TILE, depth), f32),
            own_shape,
            own_shape,
            own_shape,
        ],
        in_specs=[SMEM, VMEM, VMEM],
        out_specs=[SMEM] + [VMEM] * 4,
        scratch_shapes=[pltpu.VMEM(own_shape.shape, f32)] * 2,
        compiler_params=PARAMS,
        cost_estimate=pl.CostEstimate(flops=2**23, bytes_accessed=2**22, transcendentals=0),
        name="owned",
    )(codes, own_cond, own_field)

    def field(slots):
        return pltpu.VMEM((slots, 3, half + TILE, depth), f32)

    basis, sel = pl.pallas_call(
        basis_kernel,
        out_shape=[
            jax.ShapeDtypeStruct((layers * SLOTS * half, depth), f32),
            jax.ShapeDtypeStruct((groups, SLOTS, 128), f32),
        ],
        in_specs=[VMEM] * 8 + [hbm],
        out_specs=[VMEM, VMEM],
        scratch_shapes=[
            pltpu.VMEM((layers + 4, half + TILE, depth), f32),
            pltpu.VMEM((2, half + TILE, depth), f32),
            pltpu.VMEM((2, half + TILE, depth), f32),
            *[field(layers + 4) for _ in range(5)],
            pltpu.SMEM((count + 1,), jnp.int32),
            pltpu.SemaphoreType.DMA(()),
        ],
        compiler_params=PARAMS,
        name="basis",
    )(own_field, own_sig, own_one, own_mixed, own_twice, own_ends, first, second, listed)
    basis = basis.reshape(layers, SLOTS, half, depth)

    is_end = lax.broadcasted_iota(jnp.int32, sel.shape, 1) >= ENDS
    stride = 2
    while stride < size:
        other = lax.ppermute(sel, "space", [(i, i ^ stride) for i in range(size)])
        sel = jnp.where(is_end, jnp.maximum(sel, other), sel + other)
        stride *= 2
    ends = sel
    other = lax.ppermute(sel, "space", [(i, i ^ 1) for i in range(size)])

    cut = half - LATE
    early = [(layer, 0, half) for layer in range(layers - 1)] + [(layers - 1, 0, cut)]
    late = [(layers - 1, cut, half)]
    gated_shape = jax.ShapeDtypeStruct((gates, 3, layers, half, depth), f32)

    def buffers(number):
        return [
            pltpu.VMEM((number, gates, 3, half, depth), f32),
            pltpu.SemaphoreType.DMA((number, gates)),
        ]

    gated, w = pl.pallas_call(
        functools.partial(gate_kernel, poles=poles, blocks=early),
        out_shape=[gated_shape, jax.ShapeDtypeStruct((WORDS, 16, 128), f32)],
        in_specs=[VMEM, VMEM, VMEM],
        out_specs=[hbm, VMEM],
        scratch_shapes=buffers(len(early)),
        compiler_params=PARAMS,
        cost_estimate=pl.CostEstimate(flops=2**24, bytes_accessed=2**23, transcendentals=0),
        name="gates",
    )(ends, params, basis)

    sel, w = lax.optimization_barrier((sel + other, w))
    other = lax.ppermute(sel, "pole", [(0, 1), (1, 0)])
    gated = pl.pallas_call(
        functools.partial(rest_kernel, blocks=late),
        out_shape=gated_shape,
        in_specs=[VMEM, VMEM, hbm],
        out_specs=hbm,
        scratch_shapes=buffers(len(late)),
        input_output_aliases={2: 0},
        compiler_params=PARAMS,
        cost_estimate=pl.CostEstimate(flops=2**22, bytes_accessed=2**21, transcendentals=0),
        name="rest",
    )(w, basis, gated)
    sel = sel + other

    traces = pl.pallas_call(
        trace_kernel,
        out_shape=jax.ShapeDtypeStruct((gates, 3, count), f32),
        in_specs=[VMEM, VMEM],
        out_specs=VMEM,
        compiler_params=PARAMS,
        name="traces",
    )(w, sel)
    return gated, traces


def solution(mesh):
    placed = (
        P(("survey", "space"), None, None),
        P(None, ("survey", "space"), None, None),
        P(),
        P(),
        P("survey"),
    )
    return jax.shard_map(
        per_device,
        mesh=mesh,
        in_specs=placed,
        out_specs=(P(None, None, ("survey", "space"), "pole", None), P(None, None, "survey")),
        check_vma=False,
    )
```

```python
import functools

import jax
import jax.numpy as jnp
from jax import lax
from jax.experimental import pallas as pl
from jax.experimental.pallas import tpu as pltpu
from jax.sharding import PartitionSpec as P

MID = 4.65
WORDS = 10
POINTWISE = (0, 2, 5, 9)
FIELDS = (1, 3, 4, 6, 7, 8)
SIGMA = 3 * (1 + len(FIELDS))
ENDS = SIGMA + 1
SLOTS = ENDS + 2
GROUP = 4
LATE = 24
PICKS = 8
TILE = 8
VMEM = pl.BlockSpec(memory_space=pltpu.VMEM)
SMEM = pl.BlockSpec(memory_space=pltpu.SMEM)
PARAMS = pltpu.CompilerParams(vmem_limit_bytes=48 * 1024 * 1024)


def sub_next(v):
    return pltpu.roll(v, v.shape[0] - 1, 0)


def sub_prev(v):
    return pltpu.roll(v, 1, 0)


def lanes_of(v):
    return lax.broadcasted_iota(jnp.int32, v.shape, 1)


def rows_of(v):
    return lax.broadcasted_iota(jnp.int32, v.shape, 0)


def lane_next(v):
    return jnp.where(lanes_of(v) == v.shape[1] - 1, 0.0, pltpu.roll(v, v.shape[1] - 1, 1))


def lane_prev(v, first):
    return jnp.where(lanes_of(v) == 0, first, pltpu.roll(v, 1, 1))


def split(value, size):
    if size & (size - 1):
        return lax.div(value, size), lax.rem(value, size)
    return value >> (size.bit_length() - 1), value & (size - 1)


def bits_of(size):
    return (size - 1).bit_length()


def part_keep(core):
    row = lax.broadcasted_iota(jnp.int32, (TILE, 128), 0)
    return jnp.where(core == 0, (row < 5).astype(jnp.float32), (row >= 5).astype(jnp.float32))


def own_rows(half, core):
    return pl.ds(pl.multiple_of(core * half, TILE), half)


def extra_rows(half, core):
    return pl.ds(pl.multiple_of(half - core * TILE, TILE), TILE)


def to_front(tile, core):
    return jnp.where(core == 0, tile, pltpu.roll(tile, 3, 0))


def from_front(tile, core):
    tile = jnp.where(rows_of(tile) < 3, tile, 0.0)
    return jnp.where(core == 0, tile, pltpu.roll(tile, TILE - 3, 0))


def pack_extras(near, far, ends):
    row = rows_of(ends)
    spare = [
        pltpu.roll(far[0], 6, 0),
        pltpu.roll(far[1], 6, 0),
        jnp.where(row == 6, pltpu.roll(far[0], 4, 0), pltpu.roll(far[1], 5, 0)),
        pltpu.roll(ends, 6, 0),
    ]
    return [
        jnp.where(
            row < 3,
            near[2 * at],
            jnp.where(row < 6, pltpu.roll(near[2 * at + 1], 3, 0), spare[at]),
        )
        for at in range(4)
    ]


def unpack_near(tiles, at, core):
    tile = tiles[at // 2]
    return from_front(pltpu.roll(tile, TILE - 3, 0) if at % 2 else tile, core)


def unpack_far(tiles, at, core):
    last = pltpu.roll(tiles[2], 4 - at, 0)
    return from_front(jnp.where(rows_of(last) < 2, pltpu.roll(tiles[at], 2, 0), last), core)


def send_kernel(all_ref, first_ref, second_ref, cond_out, field_out, ends_ref):
    core = lax.axis_index("pole")
    odd = lax.rem(lax.axis_index("space"), 2)
    _, layers, rows, _ = all_ref.shape
    half = rows // 2
    own, extra = own_rows(half, core), extra_rows(half, core)
    keep = part_keep(core)
    conds, fields = [], []
    for layer in range(layers):
        *field, cond = [
            jnp.concatenate([all_ref[c, layer, own, :], all_ref[c, layer, extra, :] * keep], axis=0)
            for c in range(4)
        ]
        cond_out[layer] = cond
        for c in range(3):
            field_out[layer, c] = field[c]
        conds.append(cond)
        fields.append(field)

    top = jnp.max(jnp.max(all_ref[3], axis=0), axis=0, keepdims=True)
    low = jnp.max(-jnp.min(all_ref[3], axis=0), axis=0, keepdims=True)
    row = lax.broadcasted_iota(jnp.int32, (TILE, 128), 0)
    ends = jnp.where(row == 0, top, low)
    ends_ref[...] = ends
    for upward in (True, False):
        near = [layers - 1, layers - 2] if upward else [0, 1]
        fx, fy, fz = fields[layers - 3 if upward else 2]
        far = [fy + sub_next(fx) - fx, fz + lane_next(fx) - fx] if upward else [fy, fz]
        blocks = [v for layer in near for v in (*fields[layer], conds[layer])] + far
        edges = [to_front(block[half:], core) for block in blocks]
        pairs = pack_extras(edges[:8], edges[8:], ends)

        def write(out_ref):
            for at, block in enumerate(blocks):
                out_ref[at * half : (at + 1) * half, :] = block[:half]
            base = len(blocks) * half
            for at, pair in enumerate(pairs):
                out_ref[base + at * TILE : base + (at + 1) * TILE, :] = pair

        with_first = odd == 0 if upward else odd == 1

        @pl.when(with_first)
        def _():
            write(first_ref)

        @pl.when(jnp.logical_not(with_first))
        def _():
            write(second_ref)


def curl_curl(get_u, get, layers, put):
    first = layers[0]
    u_y, u_z = get_u(first - 1)
    _, g, e = get(first, (1, 2))
    prev_z, prev_y = g - u_y, u_z - e
    for layer in layers:
        f, g, e = get(layer, (0, 1, 2))
        _, g_up, e_up = get(layer + 1, (1, 2))
        h_z = g_up - (g + (sub_next(f) - f))
        h_y = (e + (lane_next(f) - f)) - e_up
        h_x = (sub_next(e) - e) - (lane_next(g) - g)
        out_x = (h_z - sub_prev(h_z)) + (lane_prev(h_y, f) - h_y) - 8.0 * f
        out_y = (h_x - lane_prev(h_x, -g)) + (prev_z - h_z) - 8.0 * g
        out_z = (h_y - prev_y) + (sub_prev(h_x) - h_x) - 8.0 * e
        prev_z, prev_y = h_z, h_y
        put(layer, (out_x, out_y, out_z))


def own_kernel(code_ref, cond_ref, field_ref, list_ref, sig_ref, one_ref, mixed_ref, twice_ref, t11, t22):
    layers, reach, depth = cond_ref.shape
    blank = jnp.zeros((reach, depth), jnp.float32)
    for layer in range(layers):
        moved = cond_ref[layer] - MID
        sig_ref[layer] = moved
        for c in range(3):
            once = moved * field_ref[layer, c]
            t11[layer, c] = once
            t22[layer, c] = moved * once

    def apply(src, out):
        def get(layer, which):
            if layer == layers:
                return [blank] * 3
            return [src[layer, c] if c in which else None for c in range(3)]

        def put(layer, values):
            for c in range(3):
                out[layer, c] = values[c]

        curl_curl(lambda layer: (blank, blank), get, list(range(layers)), put)

    apply(field_ref, one_ref)
    apply(t11, mixed_ref)
    apply(t22, twice_ref)

    total = code_ref.shape[0]

    def step(at, count):
        code = code_ref[at]
        list_ref[count] = code
        return count + (code >= 0).astype(jnp.int32)

    list_ref[total] = lax.fori_loop(0, total, step, jnp.int32(0), unroll=8)


def basis_kernel(
    field_ref, sig_ref, one_ref, mixed_ref, twice_ref, ends_ref, first_ref, second_ref, list_hbm,
    bas_ref, sel_ref,
    sig, low3, high3, t00, t11, t10, t20, t21, list_ref, list_sem,
):
    core = lax.axis_index("pole")
    place = lax.axis_index("space")
    odd = lax.rem(place, 2)
    layers, _, reach, depth = field_ref.shape
    half = reach - TILE
    keep = part_keep(core)
    list_copy = pltpu.make_async_copy(list_hbm, list_ref, list_sem)
    list_copy.start()
    low_ok = (place > 0).astype(jnp.float32)
    high_ok = (place < lax.axis_size("space") - 1).astype(jnp.float32)
    first, last = 2, layers + 1
    inner = list(range(first, last + 1))

    def received(upward, start, size):
        part = pl.ds(start, size)
        from_first = odd == 1 if upward else odd == 0
        return jnp.where(from_first, first_ref[part, :], second_ref[part, :])

    for upward in (True, False):
        tiles = [received(upward, 10 * half + at * TILE, TILE) for at in range(4)]
        blocks = [received(upward, at * half, half) for at in range(10)]
        near = [
            jnp.concatenate([blocks[at], unpack_near(tiles, at, core)], axis=0) for at in range(8)
        ]
        for distance in (1, 2):
            slot = first - distance if upward else last + distance
            base = (distance - 1) * 4
            moved = near[base + 3] - MID
            sig[slot] = moved
            for c in range(3):
                t00[slot, c] = near[base + c]
                t11[slot, c] = moved * near[base + c]
        far = low3 if upward else high3
        for at in range(2):
            far[at] = jnp.concatenate([blocks[8 + at], unpack_far(tiles, at, core)], axis=0)
    for slot in (first, last):
        for c in range(3):
            t11[slot, c] = sig_ref[slot - first] * field_ref[slot - first, c]

    def get_b(slot, which):
        if slot > last + 2:
            return None, high3[0], high3[1]
        if slot in inner:
            return [field_ref[slot - first, c] if c in which else None for c in range(3)]
        return [t00[slot, c] if c in which else None for c in range(3)]

    def reader(ref):
        def get(slot, which):
            return [ref[slot, c] if c in which else None for c in range(3)]

        return get

    def sums(get):
        def get_u(slot):
            if slot < 0:
                return low3[0], low3[1]
            f, g, e = get(slot, (0, 1, 2))
            return g + (sub_next(f) - f), e + (lane_next(f) - f)

        return get_u

    def inside(slot, value):
        value = jnp.concatenate([value[:half], value[half:] * keep], axis=0)
        if slot < first:
            return value * low_ok
        if slot > last:
            return value * high_ok
        return value

    def completed(part_ref, slot, get):
        out = [part_ref[slot - first, c] for c in range(3)]
        if slot == first:
            u_y, u_z = sums(get)(slot - 1)
            out[1] = out[1] - u_y
            out[2] = out[2] - u_z
        if slot == last:
            _, g, e = get(slot + 1, (1, 2))
            out[0] = out[0] + (g - sub_prev(g)) + (e - lane_prev(e, 0.0))
            out[1] = out[1] - g
            out[2] = out[2] - e
        return out

    def put_10(slot, out):
        for c in range(3):
            t10[slot, c] = inside(slot, out[c])

    def put_21(slot, out):
        moved = sig_ref[slot - first] if slot in inner else sig[slot]
        for c in range(3):
            t21[slot, c] = inside(slot, out[c]) + moved * t10[slot, c]

    def put_20(slot, out):
        for c in range(3):
            t20[slot, c] = inside(slot, out[c])

    curl_curl(sums(get_b), get_b, [0, 1], put_10)
    curl_curl(sums(get_b), get_b, [last + 1, last + 2], put_10)
    for slot in inner:
        put_10(slot, completed(one_ref, slot, get_b))
    get_11 = reader(t11)
    curl_curl(sums(get_11), get_11, [first - 1], put_21)
    curl_curl(sums(get_11), get_11, [last + 1], put_21)
    for slot in inner:
        put_21(slot, completed(mixed_ref, slot, get_11))
    get_10 = reader(t10)
    curl_curl(sums(get_10), get_10, list(range(first - 1, last + 2)), put_20)

    def store(word, slot, c, value):
        base = ((slot - first) * SLOTS + word * 3 + c) * half
        bas_ref[base : base + half, :] = value

    for slot in inner:
        for c in range(3):
            store(0, slot, c, field_ref[slot - first, c, :half, :])
            for word, ref in enumerate((t10, t20, t21), 1):
                store(word, slot, c, ref[slot, c, :half, :])
        base = ((slot - first) * SLOTS + SIGMA) * half
        bas_ref[base : base + half, :] = sig_ref[slot - first, :half, :]

    def put_3(word, before):
        def put(slot, out):
            for c in range(3):
                value = out[c][:half]
                if before is not None:
                    moved = sig_ref[slot - first, :half, :]
                    value = value + moved * before[slot, c, :half, :]
                store(word, slot, c, value)

        return put

    get_20, get_21 = reader(t20), reader(t21)
    curl_curl(sums(get_20), get_20, inner, put_3(4, None))
    curl_curl(sums(get_21), get_21, inner, put_3(5, t20))

    def get_22(slot, which):
        return [sig[slot] * t11[slot, c] if c in which else None for c in range(3)]

    for slot in inner:
        put_3(6, t21)(slot, completed(twice_ref, slot, get_22))

    groups = sel_ref.shape[0]
    lane = lax.broadcasted_iota(jnp.int32, (SLOTS, depth), 1)
    total = list_ref.shape[0] - 1
    bits = bits_of(total)
    list_copy.wait()
    owned = list_ref[total]

    def pick(turn, found):
        for step in range(PICKS):
            at = turn * PICKS + step
            code = jnp.where(at < owned, list_ref[jnp.minimum(at, total - 1)], 0)
            which = jnp.where(at < owned, code & ((1 << bits) - 1), -1)
            block = bas_ref[pl.ds(code >> (7 + bits), SLOTS, stride=half), :]
            block = pltpu.roll(block, (code >> bits) & 127, 1)
            found = [
                jnp.where(lane == which - 128 * group, block, value)
                for group, value in enumerate(found)
            ]
        return found

    zero = jnp.zeros((SLOTS, depth), jnp.float32)
    found = lax.fori_loop(0, (owned + PICKS - 1) // PICKS, pick, [zero] * groups)
    for group in range(groups):
        sel_ref[group] = found[group]

    tile = first_ref[10 * half + 3 * TILE : 10 * half + 4 * TILE, :]
    for group in range(groups):
        sel_ref[group, ENDS:, :] = jnp.maximum(ends_ref[:2, :], tile[TILE - 2 :])


def weights(ends_ref, par_ref, out_ref, gates, poles):
    upper = jnp.max(ends_ref[0, ENDS : ENDS + 1, :], axis=1, keepdims=True)
    lower = -jnp.max(ends_ref[0, ENDS + 1 : ENDS + 2, :], axis=1, keepdims=True)
    shift = jnp.where(lax.broadcasted_iota(jnp.int32, (1, 128), 1) < poles, par_ref[:1, :], 1.0)
    low_end = shift * lower
    high_end = 16.0 + shift * upper
    center = (high_end + low_end) / 2.0
    spread = (high_end - low_end) / 2.0
    scaled = center / spread
    residual = [jnp.ones_like(shift)]
    direction = [1.0 / center]
    ratio = 1.0 / scaled
    total = list(direction)
    for _ in range(3):
        applied = [center * d for d in direction] + [jnp.zeros_like(shift)]
        for at, d in enumerate(direction):
            applied[at + 1] = applied[at + 1] + spread * d
        residual = [
            (residual[at] if at < len(residual) else 0.0) - a for at, a in enumerate(applied)
        ]
        ratio_new = 1.0 / (2.0 * scaled - ratio)
        grown = [(2.0 * ratio_new / spread) * r for r in residual]
        direction = [
            g + ratio_new * ratio * direction[at] if at < len(direction) else g
            for at, g in enumerate(grown)
        ]
        ratio = ratio_new
        total = [
            d + total[at] if at < len(total) else d for at, d in enumerate(direction)
        ]
    offset = shift * (MID - (upper + lower) / 2.0)
    inverse = 1.0 / spread
    y0, y1, y2, y3 = total
    y1 = y1 * inverse
    y2 = y2 * inverse * inverse
    y3 = y3 * inverse * inverse * inverse
    powers = [
        y0 + offset * (y1 + offset * (y2 + offset * y3)),
        y1 + offset * (2.0 * y2 + 3.0 * offset * y3),
        y2 + 3.0 * offset * y3,
        y3,
    ]
    word = 0
    res = par_ref[TILE : TILE + gates, :]
    for m in range(4):
        term = powers[m]
        for _ in range(m + 1):
            column = jnp.sum(res * term, axis=1, keepdims=True)
            out_ref[word, : res.shape[0], :] = jnp.broadcast_to(column, (res.shape[0], 128))
            term = term * shift
            word += 1


def power_sum(weight, moved):
    total = weight(POINTWISE[3])
    for word in POINTWISE[2::-1]:
        total = total * moved + weight(word)
    return total


def combine(w_ref, bas_ref, out_hbm, buffer, sems, blocks):
    gates = out_hbm.shape[0]
    copies = []
    for at, (layer, begin, end) in enumerate(blocks):
        for low in range(0, gates, GROUP):
            some = range(low, min(low + GROUP, gates))
            for top in range(begin, end, TILE):
                part = slice(top, top + TILE)
                moved = bas_ref[layer, SIGMA, part, :]
                fields = [bas_ref[layer, row, part, :] for row in range(SIGMA)]
                for g in some:
                    weight = lambda word: w_ref[word, g : g + 1, :]
                    scale = power_sum(weight, moved)
                    for c in range(3):
                        total = scale * fields[c]
                        for row, word in enumerate(FIELDS, 1):
                            total = total + weight(word) * fields[row * 3 + c]
                        buffer[at, g, c, part, :] = total
            rows = pl.ds(begin, end - begin)
            for g in some:
                copy = pltpu.make_async_copy(
                    buffer.at[at, g, :, rows], out_hbm.at[g, :, layer, rows], sems.at[at, g]
                )
                copy.start()
                copies.append(copy)
    for copy in copies:
        copy.wait()


def gate_kernel(ends_ref, par_ref, bas_ref, out_hbm, w_ref, buffer, sems, *, poles, blocks):
    weights(ends_ref, par_ref, w_ref, out_hbm.shape[0], poles)
    combine(w_ref, bas_ref, out_hbm, buffer, sems, blocks)


def rest_kernel(w_ref, bas_ref, before_ref, out_hbm, buffer, sems, *, blocks):
    del before_ref
    combine(w_ref, bas_ref, out_hbm, buffer, sems, blocks)


def trace_kernel(w_ref, one_ref, other_ref, out_ref):
    gates = out_ref.shape[0]
    weight = lambda word: w_ref[word, :gates, :]
    for group in range(one_ref.shape[0]):
        sel = one_ref[group] + other_ref[group]
        scale = power_sum(weight, sel[SIGMA : SIGMA + 1])
        for c in range(3):
            total = scale * sel[c : c + 1]
            for at, word in enumerate(FIELDS, 1):
                total = total + weight(word) * sel[at * 3 + c : at * 3 + c + 1]
            for g in range(gates):
                out_ref[g, c : c + 1, group * 128 : (group + 1) * 128] = total[g : g + 1]


def per_device(conductivity, source_field, shifts, residues, receivers):
    layers, rows, depth = conductivity.shape
    half = rows // 2
    gates, poles = residues.shape
    count = receivers.shape[0]
    groups = count // 128
    size = lax.axis_size("space")
    f32 = jnp.float32
    message = jax.ShapeDtypeStruct((10 * half + 4 * TILE, depth), f32)
    hbm = pl.BlockSpec(memory_space=pltpu.HBM)

    first, second, own_cond, own_field, own_ends = pl.pallas_call(
        send_kernel,
        out_shape=[
            message,
            message,
            jax.ShapeDtypeStruct((layers, half + TILE, depth), f32),
            jax.ShapeDtypeStruct((layers, 3, half + TILE, depth), f32),
            jax.ShapeDtypeStruct((TILE, 128), f32),
        ],
        in_specs=[VMEM],
        out_specs=[VMEM] * 5,
        compiler_params=pltpu.CompilerParams(vmem_limit_bytes=48 * 1024 * 1024),
        name="send",
    )(conductivity * jnp.pad(source_field, ((0, 1), (0, 0), (0, 0), (0, 0)), constant_values=1.0))
    far_pairs = [(i, i + 1) for i in range(1, size - 1, 2)]
    far_pairs = far_pairs + [(j, i) for i, j in far_pairs]
    second = lax.ppermute(second, "space", far_pairs)
    first = lax.ppermute(first, "space", [(i, i ^ 1) for i in range(size)])

    line, z = receivers // depth, receivers % depth
    x = line // rows - lax.axis_index("space") * layers
    y = line % rows - lax.axis_index("pole") * half
    owned = (x >= 0) & (x < layers) & (y >= 0) & (y < half)
    order = lax.iota(jnp.int32, count)
    codes = (((x * (SLOTS * half) + y) << 7) | ((order - z) & 127)) << bits_of(count) | order
    codes = jnp.where(owned, codes, -1)
    params = jnp.pad(
        jnp.concatenate([jnp.pad(shifts[None], ((0, TILE - 1), (0, 0))), residues]),
        ((0, 16 - gates), (0, 128 - poles)),
    )

    own_shape = jax.ShapeDtypeStruct((layers, 3, half + TILE, depth), f32)
    listed, own_sig, own_one, own_mixed, own_twice = pl.pallas_call(
        own_kernel,
        out_shape=[
            jax.ShapeDtypeStruct((count + 1,), jnp.int32),
            jax.ShapeDtypeStruct((layers, half + TILE, depth), f32),
            own_shape,
            own_shape,
            own_shape,
        ],
        in_specs=[SMEM, VMEM, VMEM],
        out_specs=[SMEM] + [VMEM] * 4,
        scratch_shapes=[pltpu.VMEM(own_shape.shape, f32)] * 2,
        compiler_params=PARAMS,
        cost_estimate=pl.CostEstimate(flops=2**23, bytes_accessed=2**22, transcendentals=0),
        name="owned",
    )(codes, own_cond, own_field)

    def field(slots):
        return pltpu.VMEM((slots, 3, half + TILE, depth), f32)

    basis, sel = pl.pallas_call(
        basis_kernel,
        out_shape=[
            jax.ShapeDtypeStruct((layers * SLOTS * half, depth), f32),
            jax.ShapeDtypeStruct((groups, SLOTS, 128), f32),
        ],
        in_specs=[VMEM] * 8 + [hbm],
        out_specs=[VMEM, VMEM],
        scratch_shapes=[
            pltpu.VMEM((layers + 4, half + TILE, depth), f32),
            pltpu.VMEM((2, half + TILE, depth), f32),
            pltpu.VMEM((2, half + TILE, depth), f32),
            *[field(layers + 4) for _ in range(5)],
            pltpu.SMEM((count + 1,), jnp.int32),
            pltpu.SemaphoreType.DMA(()),
        ],
        compiler_params=PARAMS,
        name="basis",
    )(own_field, own_sig, own_one, own_mixed, own_twice, own_ends, first, second, listed)
    basis = basis.reshape(layers, SLOTS, half, depth)

    is_end = lax.broadcasted_iota(jnp.int32, sel.shape, 1) >= ENDS
    stride = 2
    while stride < size:
        other = lax.ppermute(sel, "space", [(i, i ^ stride) for i in range(size)])
        sel = jnp.where(is_end, jnp.maximum(sel, other), sel + other)
        stride *= 2
    ends = sel
    other = lax.ppermute(sel, "space", [(i, i ^ 1) for i in range(size)])

    cut = half - LATE
    early = [(layer, 0, half) for layer in range(layers - 1)] + [(layers - 1, 0, cut)]
    late = [(layers - 1, cut, half)]
    gated_shape = jax.ShapeDtypeStruct((gates, 3, layers, half, depth), f32)

    def buffers(number):
        return [
            pltpu.VMEM((number, gates, 3, half, depth), f32),
            pltpu.SemaphoreType.DMA((number, gates)),
        ]

    gated, w = pl.pallas_call(
        functools.partial(gate_kernel, poles=poles, blocks=early),
        out_shape=[gated_shape, jax.ShapeDtypeStruct((WORDS, 16, 128), f32)],
        in_specs=[VMEM, VMEM, VMEM],
        out_specs=[hbm, VMEM],
        scratch_shapes=buffers(len(early)),
        compiler_params=PARAMS,
        cost_estimate=pl.CostEstimate(flops=2**24, bytes_accessed=2**23, transcendentals=0),
        name="gates",
    )(ends, params, basis)

    sel, w = lax.optimization_barrier((sel + other, w))
    other = lax.ppermute(sel, "pole", [(0, 1), (1, 0)])
    gated = pl.pallas_call(
        functools.partial(rest_kernel, blocks=late),
        out_shape=gated_shape,
        in_specs=[VMEM, VMEM, hbm],
        out_specs=hbm,
        scratch_shapes=buffers(len(late)),
        input_output_aliases={2: 0},
        compiler_params=PARAMS,
        cost_estimate=pl.CostEstimate(flops=2**22, bytes_accessed=2**21, transcendentals=0),
        name="rest",
    )(w, basis, gated)
    traces = pl.pallas_call(
        trace_kernel,
        out_shape=jax.ShapeDtypeStruct((gates, 3, count), f32),
        in_specs=[VMEM, VMEM, VMEM],
        out_specs=VMEM,
        compiler_params=PARAMS,
        name="traces",
    )(w, sel, other)
    return gated, traces


def solution(mesh):
    placed = (
        P(("survey", "space"), None, None),
        P(None, ("survey", "space"), None, None),
        P(),
        P(),
        P("survey"),
    )
    return jax.shard_map(
        per_device,
        mesh=mesh,
        in_specs=placed,
        out_specs=(P(None, None, ("survey", "space"), "pole", None), P(None, None, "survey")),
        check_vma=False,
    )
```

```python
import functools

import jax
import jax.numpy as jnp
from jax import lax
from jax.experimental import pallas as pl
from jax.experimental.pallas import tpu as pltpu
from jax.sharding import PartitionSpec as P

MID = 4.65
WORDS = 10
POINTWISE = (0, 2, 5, 9)
FIELDS = (1, 3, 4, 6, 7, 8)
SIGMA = 3 * (1 + len(FIELDS))
ENDS = SIGMA + 1
SLOTS = ENDS + 2
GROUP = 4
LATE = 24
PICKS = 8
TILE = 8
VMEM = pl.BlockSpec(memory_space=pltpu.VMEM)
SMEM = pl.BlockSpec(memory_space=pltpu.SMEM)
PARAMS = pltpu.CompilerParams(vmem_limit_bytes=48 * 1024 * 1024)


def sub_next(v):
    return pltpu.roll(v, v.shape[0] - 1, 0)


def sub_prev(v):
    return pltpu.roll(v, 1, 0)


def lanes_of(v):
    return lax.broadcasted_iota(jnp.int32, v.shape, 1)


def rows_of(v):
    return lax.broadcasted_iota(jnp.int32, v.shape, 0)


def lane_next(v):
    return jnp.where(lanes_of(v) == v.shape[1] - 1, 0.0, pltpu.roll(v, v.shape[1] - 1, 1))


def lane_prev(v, first):
    return jnp.where(lanes_of(v) == 0, first, pltpu.roll(v, 1, 1))


def split(value, size):
    if size & (size - 1):
        return lax.div(value, size), lax.rem(value, size)
    return value >> (size.bit_length() - 1), value & (size - 1)


def bits_of(size):
    return (size - 1).bit_length()


def part_keep(core):
    row = lax.broadcasted_iota(jnp.int32, (TILE, 128), 0)
    return jnp.where(core == 0, (row < 5).astype(jnp.float32), (row >= 5).astype(jnp.float32))


def own_rows(half, core):
    return pl.ds(pl.multiple_of(core * half, TILE), half)


def extra_rows(half, core):
    return pl.ds(pl.multiple_of(half - core * TILE, TILE), TILE)


def to_front(tile, core):
    return jnp.where(core == 0, tile, pltpu.roll(tile, 3, 0))


def from_front(tile, core):
    tile = jnp.where(rows_of(tile) < 3, tile, 0.0)
    return jnp.where(core == 0, tile, pltpu.roll(tile, TILE - 3, 0))


def pack_extras(near, far, ends):
    row = rows_of(ends)
    spare = [
        pltpu.roll(far[0], 6, 0),
        pltpu.roll(far[1], 6, 0),
        jnp.where(row == 6, pltpu.roll(far[0], 4, 0), pltpu.roll(far[1], 5, 0)),
        pltpu.roll(ends, 6, 0),
    ]
    return [
        jnp.where(
            row < 3,
            near[2 * at],
            jnp.where(row < 6, pltpu.roll(near[2 * at + 1], 3, 0), spare[at]),
        )
        for at in range(4)
    ]


def unpack_near(tiles, at, core):
    tile = tiles[at // 2]
    return from_front(pltpu.roll(tile, TILE - 3, 0) if at % 2 else tile, core)


def unpack_far(tiles, at, core):
    last = pltpu.roll(tiles[2], 4 - at, 0)
    return from_front(jnp.where(rows_of(last) < 2, pltpu.roll(tiles[at], 2, 0), last), core)


def send_kernel(all_ref, first_ref, second_ref, cond_out, field_out, ends_ref):
    core = lax.axis_index("pole")
    odd = lax.rem(lax.axis_index("space"), 2)
    _, layers, rows, _ = all_ref.shape
    half = rows // 2
    own, extra = own_rows(half, core), extra_rows(half, core)
    keep = part_keep(core)
    conds, fields = [], []
    for layer in range(layers):
        *field, cond = [
            jnp.concatenate([all_ref[c, layer, own, :], all_ref[c, layer, extra, :] * keep], axis=0)
            for c in range(4)
        ]
        cond_out[layer] = cond
        for c in range(3):
            field_out[layer, c] = field[c]
        conds.append(cond)
        fields.append(field)

    top = jnp.max(jnp.max(all_ref[3], axis=0), axis=0, keepdims=True)
    low = jnp.max(-jnp.min(all_ref[3], axis=0), axis=0, keepdims=True)
    row = lax.broadcasted_iota(jnp.int32, (TILE, 128), 0)
    ends = jnp.where(row == 0, top, low)
    ends_ref[...] = ends
    for upward in (True, False):
        near = [layers - 1, layers - 2] if upward else [0, 1]
        fx, fy, fz = fields[layers - 3 if upward else 2]
        far = [fy + sub_next(fx) - fx, fz + lane_next(fx) - fx] if upward else [fy, fz]
        blocks = [v for layer in near for v in (*fields[layer], conds[layer])] + far
        edges = [to_front(block[half:], core) for block in blocks]
        pairs = pack_extras(edges[:8], edges[8:], ends)

        def write(out_ref):
            for at, block in enumerate(blocks):
                out_ref[at * half : (at + 1) * half, :] = block[:half]
            base = len(blocks) * half
            for at, pair in enumerate(pairs):
                out_ref[base + at * TILE : base + (at + 1) * TILE, :] = pair

        with_first = odd == 0 if upward else odd == 1

        @pl.when(with_first)
        def _():
            write(first_ref)

        @pl.when(jnp.logical_not(with_first))
        def _():
            write(second_ref)


def curl_curl(get_u, get, layers, put):
    first = layers[0]
    u_y, u_z = get_u(first - 1)
    _, g, e = get(first, (1, 2))
    prev_z, prev_y = g - u_y, u_z - e
    for layer in layers:
        f, g, e = get(layer, (0, 1, 2))
        _, g_up, e_up = get(layer + 1, (1, 2))
        h_z = g_up - (g + (sub_next(f) - f))
        h_y = (e + (lane_next(f) - f)) - e_up
        h_x = (sub_next(e) - e) - (lane_next(g) - g)
        out_x = (h_z - sub_prev(h_z)) + (lane_prev(h_y, f) - h_y) - 8.0 * f
        out_y = (h_x - lane_prev(h_x, -g)) + (prev_z - h_z) - 8.0 * g
        out_z = (h_y - prev_y) + (sub_prev(h_x) - h_x) - 8.0 * e
        prev_z, prev_y = h_z, h_y
        put(layer, (out_x, out_y, out_z))


def own_kernel(code_ref, cond_ref, field_ref, list_ref, sig_ref, one_ref, mixed_ref, twice_ref, t11, t22):
    layers, reach, depth = cond_ref.shape
    blank = jnp.zeros((reach, depth), jnp.float32)
    for layer in range(layers):
        moved = cond_ref[layer] - MID
        sig_ref[layer] = moved
        for c in range(3):
            once = moved * field_ref[layer, c]
            t11[layer, c] = once
            t22[layer, c] = moved * once

    def apply(src, out):
        def get(layer, which):
            if layer == layers:
                return [blank] * 3
            return [src[layer, c] if c in which else None for c in range(3)]

        def put(layer, values):
            for c in range(3):
                out[layer, c] = values[c]

        curl_curl(lambda layer: (blank, blank), get, list(range(layers)), put)

    apply(field_ref, one_ref)
    apply(t11, mixed_ref)
    apply(t22, twice_ref)
    keep = part_keep(lax.axis_index("pole"))
    half = reach - TILE
    for layer in range(1, layers - 1):
        for c in range(3):
            one = one_ref[layer, c]
            one = jnp.concatenate([one[:half], one[half:] * keep], axis=0)
            one_ref[layer, c] = one
            mixed = mixed_ref[layer, c]
            mixed = jnp.concatenate([mixed[:half], mixed[half:] * keep], axis=0)
            mixed_ref[layer, c] = mixed + sig_ref[layer] * one

    total = code_ref.shape[0]

    def step(at, count):
        code = code_ref[at]
        list_ref[count] = code
        return count + (code >= 0).astype(jnp.int32)

    list_ref[total] = lax.fori_loop(0, total, step, jnp.int32(0), unroll=8)


def basis_kernel(
    field_ref, sig_ref, one_ref, mixed_ref, twice_ref, ends_ref, first_ref, second_ref, list_hbm,
    bas_ref, sel_ref,
    sig, low3, high3, t00, t11, t10, t20, t21, list_ref, list_sem,
):
    core = lax.axis_index("pole")
    place = lax.axis_index("space")
    odd = lax.rem(place, 2)
    layers, _, reach, depth = field_ref.shape
    half = reach - TILE
    keep = part_keep(core)
    list_copy = pltpu.make_async_copy(list_hbm, list_ref, list_sem)
    list_copy.start()
    low_ok = (place > 0).astype(jnp.float32)
    high_ok = (place < lax.axis_size("space") - 1).astype(jnp.float32)
    first, last = 2, layers + 1
    inner = list(range(first, last + 1))

    def received(upward, start, size):
        part = pl.ds(start, size)
        from_first = odd == 1 if upward else odd == 0
        return jnp.where(from_first, first_ref[part, :], second_ref[part, :])

    for upward in (True, False):
        tiles = [received(upward, 10 * half + at * TILE, TILE) for at in range(4)]
        blocks = [received(upward, at * half, half) for at in range(10)]
        near = [
            jnp.concatenate([blocks[at], unpack_near(tiles, at, core)], axis=0) for at in range(8)
        ]
        for distance in (1, 2):
            slot = first - distance if upward else last + distance
            base = (distance - 1) * 4
            moved = near[base + 3] - MID
            sig[slot] = moved
            for c in range(3):
                t00[slot, c] = near[base + c]
                t11[slot, c] = moved * near[base + c]
        far = low3 if upward else high3
        for at in range(2):
            far[at] = jnp.concatenate([blocks[8 + at], unpack_far(tiles, at, core)], axis=0)
    for slot in (first, last):
        for c in range(3):
            t11[slot, c] = sig_ref[slot - first] * field_ref[slot - first, c]

    def get_b(slot, which):
        if slot > last + 2:
            return None, high3[0], high3[1]
        if slot in inner:
            return [field_ref[slot - first, c] if c in which else None for c in range(3)]
        return [t00[slot, c] if c in which else None for c in range(3)]

    def reader(ref):
        def get(slot, which):
            return [ref[slot, c] if c in which else None for c in range(3)]

        return get

    def view(ref, own_ref, slot):
        return (own_ref, slot - first) if first < slot < last else (ref, slot)

    def mixed_reader(ref, own_ref):
        def get(slot, which):
            array, at = view(ref, own_ref, slot)
            return [array[at, c] if c in which else None for c in range(3)]

        return get

    def sums(get):
        def get_u(slot):
            if slot < 0:
                return low3[0], low3[1]
            f, g, e = get(slot, (0, 1, 2))
            return g + (sub_next(f) - f), e + (lane_next(f) - f)

        return get_u

    def inside(slot, value):
        value = jnp.concatenate([value[:half], value[half:] * keep], axis=0)
        if slot < first:
            return value * low_ok
        if slot > last:
            return value * high_ok
        return value

    def completed(part_ref, slot, get):
        out = [part_ref[slot - first, c] for c in range(3)]
        if slot == first:
            u_y, u_z = sums(get)(slot - 1)
            out[1] = out[1] - u_y
            out[2] = out[2] - u_z
        if slot == last:
            _, g, e = get(slot + 1, (1, 2))
            out[0] = out[0] + (g - sub_prev(g)) + (e - lane_prev(e, 0.0))
            out[1] = out[1] - g
            out[2] = out[2] - e
        return out

    def put_10(slot, out):
        for c in range(3):
            t10[slot, c] = inside(slot, out[c])

    def put_21(slot, out):
        moved = sig_ref[slot - first] if slot in inner else sig[slot]
        for c in range(3):
            t21[slot, c] = inside(slot, out[c]) + moved * t10[slot, c]

    def put_20(slot, out):
        for c in range(3):
            t20[slot, c] = inside(slot, out[c])

    curl_curl(sums(get_b), get_b, [0, 1], put_10)
    curl_curl(sums(get_b), get_b, [last + 1, last + 2], put_10)
    for slot in (first, last):
        put_10(slot, completed(one_ref, slot, get_b))
    get_11 = reader(t11)
    curl_curl(sums(get_11), get_11, [first - 1], put_21)
    curl_curl(sums(get_11), get_11, [last + 1], put_21)
    for slot in (first, last):
        put_21(slot, completed(mixed_ref, slot, get_11))
    get_10 = mixed_reader(t10, one_ref)
    curl_curl(sums(get_10), get_10, list(range(first - 1, last + 2)), put_20)

    def store(word, slot, c, value):
        base = ((slot - first) * SLOTS + word * 3 + c) * half
        bas_ref[base : base + half, :] = value

    for slot in inner:
        for c in range(3):
            store(0, slot, c, field_ref[slot - first, c, :half, :])
            for word, (ref, at) in enumerate(
                (view(t10, one_ref, slot), (t20, slot), view(t21, mixed_ref, slot)), 1
            ):
                store(word, slot, c, ref[at, c, :half, :])
        base = ((slot - first) * SLOTS + SIGMA) * half
        bas_ref[base : base + half, :] = sig_ref[slot - first, :half, :]

    def put_3(word, before):
        def put(slot, out):
            for c in range(3):
                value = out[c][:half]
                if before is not None:
                    moved = sig_ref[slot - first, :half, :]
                    ref, at = before(slot)
                    value = value + moved * ref[at, c, :half, :]
                store(word, slot, c, value)

        return put

    get_20, get_21 = reader(t20), mixed_reader(t21, mixed_ref)
    curl_curl(sums(get_20), get_20, inner, put_3(4, None))
    curl_curl(sums(get_21), get_21, inner, put_3(5, lambda slot: (t20, slot)))

    def get_22(slot, which):
        return [sig[slot] * t11[slot, c] if c in which else None for c in range(3)]

    for slot in inner:
        put_3(6, lambda slot: view(t21, mixed_ref, slot))(slot, completed(twice_ref, slot, get_22))

    groups = sel_ref.shape[0]
    lane = lax.broadcasted_iota(jnp.int32, (SLOTS, depth), 1)
    total = list_ref.shape[0] - 1
    bits = bits_of(total)
    list_copy.wait()
    owned = list_ref[total]

    def pick(turn, found):
        for step in range(PICKS):
            at = turn * PICKS + step
            code = jnp.where(at < owned, list_ref[jnp.minimum(at, total - 1)], 0)
            which = jnp.where(at < owned, code & ((1 << bits) - 1), -1)
            block = bas_ref[pl.ds(code >> (7 + bits), SLOTS, stride=half), :]
            block = pltpu.roll(block, (code >> bits) & 127, 1)
            found = [
                jnp.where(lane == which - 128 * group, block, value)
                for group, value in enumerate(found)
            ]
        return found

    zero = jnp.zeros((SLOTS, depth), jnp.float32)
    found = lax.fori_loop(0, (owned + PICKS - 1) // PICKS, pick, [zero] * groups)
    for group in range(groups):
        sel_ref[group] = found[group]

    tile = first_ref[10 * half + 3 * TILE : 10 * half + 4 * TILE, :]
    for group in range(groups):
        sel_ref[group, ENDS:, :] = jnp.maximum(ends_ref[:2, :], tile[TILE - 2 :])


def weights(ends_ref, par_ref, out_ref, gates, poles):
    upper = jnp.max(ends_ref[0, ENDS : ENDS + 1, :], axis=1, keepdims=True)
    lower = -jnp.max(ends_ref[0, ENDS + 1 : ENDS + 2, :], axis=1, keepdims=True)
    shift = jnp.where(lax.broadcasted_iota(jnp.int32, (1, 128), 1) < poles, par_ref[:1, :], 1.0)
    low_end = shift * lower
    high_end = 16.0 + shift * upper
    center = (high_end + low_end) / 2.0
    spread = (high_end - low_end) / 2.0
    scaled = center / spread
    residual = [jnp.ones_like(shift)]
    direction = [1.0 / center]
    ratio = 1.0 / scaled
    total = list(direction)
    for _ in range(3):
        applied = [center * d for d in direction] + [jnp.zeros_like(shift)]
        for at, d in enumerate(direction):
            applied[at + 1] = applied[at + 1] + spread * d
        residual = [
            (residual[at] if at < len(residual) else 0.0) - a for at, a in enumerate(applied)
        ]
        ratio_new = 1.0 / (2.0 * scaled - ratio)
        grown = [(2.0 * ratio_new / spread) * r for r in residual]
        direction = [
            g + ratio_new * ratio * direction[at] if at < len(direction) else g
            for at, g in enumerate(grown)
        ]
        ratio = ratio_new
        total = [
            d + total[at] if at < len(total) else d for at, d in enumerate(direction)
        ]
    offset = shift * (MID - (upper + lower) / 2.0)
    inverse = 1.0 / spread
    y0, y1, y2, y3 = total
    y1 = y1 * inverse
    y2 = y2 * inverse * inverse
    y3 = y3 * inverse * inverse * inverse
    powers = [
        y0 + offset * (y1 + offset * (y2 + offset * y3)),
        y1 + offset * (2.0 * y2 + 3.0 * offset * y3),
        y2 + 3.0 * offset * y3,
        y3,
    ]
    word = 0
    res = par_ref[TILE : TILE + gates, :]
    for m in range(4):
        term = powers[m]
        for _ in range(m + 1):
            column = jnp.sum(res * term, axis=1, keepdims=True)
            out_ref[word, : res.shape[0], :] = jnp.broadcast_to(column, (res.shape[0], 128))
            term = term * shift
            word += 1


def power_sum(weight, moved):
    total = weight(POINTWISE[3])
    for word in POINTWISE[2::-1]:
        total = total * moved + weight(word)
    return total


def combine(w_ref, bas_ref, out_hbm, buffer, sems, blocks):
    gates = out_hbm.shape[0]
    copies = []
    for at, (layer, begin, end) in enumerate(blocks):
        for low in range(0, gates, GROUP):
            some = range(low, min(low + GROUP, gates))
            for top in range(begin, end, TILE):
                part = slice(top, top + TILE)
                moved = bas_ref[layer, SIGMA, part, :]
                fields = [bas_ref[layer, row, part, :] for row in range(SIGMA)]
                for g in some:
                    weight = lambda word: w_ref[word, g : g + 1, :]
                    scale = power_sum(weight, moved)
                    for c in range(3):
                        total = scale * fields[c]
                        for row, word in enumerate(FIELDS, 1):
                            total = total + weight(word) * fields[row * 3 + c]
                        buffer[at, g, c, part, :] = total
            rows = pl.ds(begin, end - begin)
            for g in some:
                copy = pltpu.make_async_copy(
                    buffer.at[at, g, :, rows], out_hbm.at[g, :, layer, rows], sems.at[at, g]
                )
                copy.start()
                copies.append(copy)
    for copy in copies:
        copy.wait()


def gate_kernel(ends_ref, par_ref, bas_ref, out_hbm, w_ref, buffer, sems, *, poles, blocks):
    weights(ends_ref, par_ref, w_ref, out_hbm.shape[0], poles)
    combine(w_ref, bas_ref, out_hbm, buffer, sems, blocks)


def rest_kernel(w_ref, bas_ref, before_ref, out_hbm, buffer, sems, *, blocks):
    del before_ref
    combine(w_ref, bas_ref, out_hbm, buffer, sems, blocks)


def trace_kernel(w_ref, one_ref, other_ref, out_ref):
    gates = out_ref.shape[0]
    weight = lambda word: w_ref[word, :gates, :]
    for group in range(one_ref.shape[0]):
        sel = one_ref[group] + other_ref[group]
        scale = power_sum(weight, sel[SIGMA : SIGMA + 1])
        for c in range(3):
            total = scale * sel[c : c + 1]
            for at, word in enumerate(FIELDS, 1):
                total = total + weight(word) * sel[at * 3 + c : at * 3 + c + 1]
            for g in range(gates):
                out_ref[g, c : c + 1, group * 128 : (group + 1) * 128] = total[g : g + 1]


def per_device(conductivity, source_field, shifts, residues, receivers):
    layers, rows, depth = conductivity.shape
    half = rows // 2
    gates, poles = residues.shape
    count = receivers.shape[0]
    groups = count // 128
    size = lax.axis_size("space")
    f32 = jnp.float32
    message = jax.ShapeDtypeStruct((10 * half + 4 * TILE, depth), f32)
    hbm = pl.BlockSpec(memory_space=pltpu.HBM)

    first, second, own_cond, own_field, own_ends = pl.pallas_call(
        send_kernel,
        out_shape=[
            message,
            message,
            jax.ShapeDtypeStruct((layers, half + TILE, depth), f32),
            jax.ShapeDtypeStruct((layers, 3, half + TILE, depth), f32),
            jax.ShapeDtypeStruct((TILE, 128), f32),
        ],
        in_specs=[VMEM],
        out_specs=[VMEM] * 5,
        compiler_params=pltpu.CompilerParams(vmem_limit_bytes=48 * 1024 * 1024),
        name="send",
    )(conductivity * jnp.pad(source_field, ((0, 1), (0, 0), (0, 0), (0, 0)), constant_values=1.0))
    far_pairs = [(i, i + 1) for i in range(1, size - 1, 2)]
    far_pairs = far_pairs + [(j, i) for i, j in far_pairs]
    second = lax.ppermute(second, "space", far_pairs)
    first = lax.ppermute(first, "space", [(i, i ^ 1) for i in range(size)])

    line, z = receivers // depth, receivers % depth
    x = line // rows - lax.axis_index("space") * layers
    y = line % rows - lax.axis_index("pole") * half
    owned = (x >= 0) & (x < layers) & (y >= 0) & (y < half)
    order = lax.iota(jnp.int32, count)
    codes = (((x * (SLOTS * half) + y) << 7) | ((order - z) & 127)) << bits_of(count) | order
    codes = jnp.where(owned, codes, -1)
    params = jnp.pad(
        jnp.concatenate([jnp.pad(shifts[None], ((0, TILE - 1), (0, 0))), residues]),
        ((0, 16 - gates), (0, 128 - poles)),
    )

    own_shape = jax.ShapeDtypeStruct((layers, 3, half + TILE, depth), f32)
    listed, own_sig, own_one, own_mixed, own_twice = pl.pallas_call(
        own_kernel,
        out_shape=[
            jax.ShapeDtypeStruct((count + 1,), jnp.int32),
            jax.ShapeDtypeStruct((layers, half + TILE, depth), f32),
            own_shape,
            own_shape,
            own_shape,
        ],
        in_specs=[SMEM, VMEM, VMEM],
        out_specs=[SMEM] + [VMEM] * 4,
        scratch_shapes=[pltpu.VMEM(own_shape.shape, f32)] * 2,
        compiler_params=PARAMS,
        cost_estimate=pl.CostEstimate(flops=2**23, bytes_accessed=2**22, transcendentals=0),
        name="owned",
    )(codes, own_cond, own_field)

    def field(slots):
        return pltpu.VMEM((slots, 3, half + TILE, depth), f32)

    basis, sel = pl.pallas_call(
        basis_kernel,
        out_shape=[
            jax.ShapeDtypeStruct((layers * SLOTS * half, depth), f32),
            jax.ShapeDtypeStruct((groups, SLOTS, 128), f32),
        ],
        in_specs=[VMEM] * 8 + [hbm],
        out_specs=[VMEM, VMEM],
        scratch_shapes=[
            pltpu.VMEM((layers + 4, half + TILE, depth), f32),
            pltpu.VMEM((2, half + TILE, depth), f32),
            pltpu.VMEM((2, half + TILE, depth), f32),
            *[field(layers + 4) for _ in range(5)],
            pltpu.SMEM((count + 1,), jnp.int32),
            pltpu.SemaphoreType.DMA(()),
        ],
        compiler_params=PARAMS,
        name="basis",
    )(own_field, own_sig, own_one, own_mixed, own_twice, own_ends, first, second, listed)
    basis = basis.reshape(layers, SLOTS, half, depth)

    is_end = lax.broadcasted_iota(jnp.int32, sel.shape, 1) >= ENDS
    stride = 2
    while stride < size:
        other = lax.ppermute(sel, "space", [(i, i ^ stride) for i in range(size)])
        sel = jnp.where(is_end, jnp.maximum(sel, other), sel + other)
        stride *= 2
    ends = sel
    other = lax.ppermute(sel, "space", [(i, i ^ 1) for i in range(size)])

    cut = half - LATE
    early = [(layer, 0, half) for layer in range(layers - 1)] + [(layers - 1, 0, cut)]
    late = [(layers - 1, cut, half)]
    gated_shape = jax.ShapeDtypeStruct((gates, 3, layers, half, depth), f32)

    def buffers(number):
        return [
            pltpu.VMEM((number, gates, 3, half, depth), f32),
            pltpu.SemaphoreType.DMA((number, gates)),
        ]

    gated, w = pl.pallas_call(
        functools.partial(gate_kernel, poles=poles, blocks=early),
        out_shape=[gated_shape, jax.ShapeDtypeStruct((WORDS, 16, 128), f32)],
        in_specs=[VMEM, VMEM, VMEM],
        out_specs=[hbm, VMEM],
        scratch_shapes=buffers(len(early)),
        compiler_params=PARAMS,
        cost_estimate=pl.CostEstimate(flops=2**24, bytes_accessed=2**23, transcendentals=0),
        name="gates",
    )(ends, params, basis)

    sel, w = lax.optimization_barrier((sel + other, w))
    other = lax.ppermute(sel, "pole", [(0, 1), (1, 0)])
    gated = pl.pallas_call(
        functools.partial(rest_kernel, blocks=late),
        out_shape=gated_shape,
        in_specs=[VMEM, VMEM, hbm],
        out_specs=hbm,
        scratch_shapes=buffers(len(late)),
        input_output_aliases={2: 0},
        compiler_params=PARAMS,
        cost_estimate=pl.CostEstimate(flops=2**22, bytes_accessed=2**21, transcendentals=0),
        name="rest",
    )(w, basis, gated)
    traces = pl.pallas_call(
        trace_kernel,
        out_shape=jax.ShapeDtypeStruct((gates, 3, count), f32),
        in_specs=[VMEM, VMEM, VMEM],
        out_specs=VMEM,
        compiler_params=PARAMS,
        name="traces",
    )(w, sel, other)
    return gated, traces


def solution(mesh):
    placed = (
        P(("survey", "space"), None, None),
        P(None, ("survey", "space"), None, None),
        P(),
        P(),
        P("survey"),
    )
    return jax.shard_map(
        per_device,
        mesh=mesh,
        in_specs=placed,
        out_specs=(P(None, None, ("survey", "space"), "pole", None), P(None, None, "survey")),
        check_vma=False,
    )
```
